128 devices in a mesh: section: 16 (over y, x_hi, core), tensor: 8 (over x_lo, z).
Axes of the slice: x: 4 (x_hi: 2, x_lo: 2; x = x_hi * 2 + x_lo), y: 4, z: 4, core: 2. Of those that a mesh axis runs over, the one named last changes fastest.
Arguments:
- section_input: bfloat16 [16, 256, 8192], P('section', 'tensor')
- positions: int32 [16, 256], P('section'), may hold values from 0 to 127, as said below
- attn_gain: bfloat16 [16, 8192], P('section'), may hold values from 0.099609375 to 1.8984375
- w_query: bfloat16 [16, 8192, 4096], P('section', None, 'tensor')
- w_keyval: bfloat16 [16, 8192, 8, 256], P('section', None, 'tensor')
- w_out_proj: bfloat16 [16, 4096, 8192], P('section', 'tensor'), may hold values from -0.09375 to 0.09375
- final_gain: bfloat16 [8192], replicated, may hold values from 0.099609375 to 1.8984375
- w_vocab: bfloat16 [8192, 32768], P(None, ('section', 'tensor'))
- targets: int32 [256], replicated, may hold values from 0 to 32767
Outputs:
- handed: bfloat16 [16, 256, 8192], P('section', 'tensor')
- logprob: float32 [256], P('tensor')
The draws below stay inside these ranges and needn't reach their ends.
Inputs may be any that keep to these rules, and one draw needn't show every extreme that they name: positions[s, i] counts the tokens since the start of token i's document; documents are packed in microbatches of 128 tokens, every microbatch starts one at its first token, and in every draw some microbatch is a single document.
All inputs are finite; a program needn't handle non-finite values.
Results may differ from the reference program's by a relative error of at most 0.011.
Values may be sent and summed in bfloat16 or wider, within the bound.
No kernel may reach another device: no remote copies, remote signals or barrier semaphores. Data moves between devices by JAX's collectives and lax.ppermute only.
A program may use at most 128 MiB of HBM per device.

```python
import math
import jax
import jax.numpy as jnp
import numpy as np
from jax import lax

D = 8192
HEAD_DIM = 128
QH = 32
KVH = 8
MB_TOK = 128
MICRO = 2
TOKENS = 256
VOCAB = 32768
N_SECTION = 16


def spread_scales(scale_key, array_shape, lowest, highest):
    return jnp.exp(jax.random.uniform(scale_key, array_shape, jnp.float32, math.log(lowest), math.log(highest)))


def draw_positions(key, part):
    key = jax.random.fold_in(key, 11)
    flag_key, pick_key = jax.random.split(key)
    token_index = jnp.arange(TOKENS, dtype=jnp.int32)
    inside = token_index % MB_TOK
    starts = (jax.random.randint(flag_key, (N_SECTION, TOKENS), 0, 40) == 0) | (inside == 0)[None, :]
    single = jax.random.randint(pick_key, (), 0, N_SECTION * MICRO)
    batch_id = jnp.arange(N_SECTION, dtype=jnp.int32)[:, None] * MICRO + (token_index // MB_TOK)[None, :]
    starts = jnp.where((batch_id == single) & (inside != 0)[None, :], False, starts)
    start_marks = jnp.where(starts, token_index[None, :], 0)
    return (token_index[None, :] - lax.cummax(start_marks, axis=1)).astype(jnp.int32)


def draw_section_input(key, part):
    key = jax.random.fold_in(key, 3)
    subkeys = jax.random.split(key, 3)
    array_shape = (N_SECTION, TOKENS, D)
    row_scale = spread_scales(subkeys[1], (N_SECTION, TOKENS, 1), 0.3, 3.0)
    col_scale = spread_scales(subkeys[2], (1, 1, D), 0.3, 3.0)
    values = jax.random.normal(subkeys[0], array_shape, jnp.float32)
    return (values * row_scale * col_scale).astype(jnp.bfloat16)


def draw_w_query(key, part):
    key = jax.random.fold_in(key, 5)
    main_key = jax.random.fold_in(key, 0)
    values = jax.random.normal(main_key, (N_SECTION, D, QH, HEAD_DIM), jnp.float32) / math.sqrt(D)
    return values.reshape(N_SECTION, D, QH * HEAD_DIM).astype(jnp.bfloat16)


def draw_w_keyval(key, part):
    key = jax.random.fold_in(key, 7)
    main_key = jax.random.fold_in(key, 0)
    values = jax.random.normal(main_key, (N_SECTION, D, KVH, 2 * HEAD_DIM), jnp.float32) / math.sqrt(D)
    return values.astype(jnp.bfloat16)


def draw_w_vocab(key, part):
    key = jax.random.fold_in(key, 9)
    subkeys = jax.random.split(key, 1)
    col_scale = math.sqrt(12.0 / D)
    values = jax.random.normal(subkeys[0], (D, VOCAB), jnp.float32) * col_scale
    return values.astype(jnp.bfloat16)


def set_ends(array, key, least, largest):
    dims = array.shape
    index_at = [jax.random.randint(jax.random.fold_in(key, axis), (), 0, dims[axis]) for axis in range(len(dims))]
    array = array.at[tuple(index_at)].set(least)
    longest = dims.index(max(dims))
    index_at[longest] = (index_at[longest] + 1) % dims[longest]
    return array.at[tuple(index_at)].set(largest)


def block_levels(stream_key, shape, cuts, smallest, largest):
    gain, own = 1.0, jax.random.fold_in(stream_key, 6)
    for axis_at, parts in cuts:
        heights = jnp.exp(jax.random.uniform(jax.random.fold_in(own, axis_at), (parts,), jnp.float32, smallest / len(cuts), largest / len(cuts)))
        gain = gain * jnp.repeat(heights, shape[axis_at] // parts).reshape([-1 if axis == axis_at else 1 for axis in range(len(shape))])
    return gain


def rank_bounds(number_of, slope):
    weights = [(1 << 20) // math.isqrt(rank ** slope) + 1 for rank in range(1, number_of + 1)]
    deviation = 1 + sum(weights) // (1 << 30)
    return np.cumsum(np.array([max(1, weight // deviation) for weight in weights]))


def ranked(key, shape, count, skew):
    table = rank_bounds(count, skew)
    lot = jax.random.randint(jax.random.fold_in(key, 1), shape, 0, int(table[count - 1]))
    rank = jnp.searchsorted(jnp.asarray(table, jnp.int32), lot, side="right")
    return jax.random.permutation(jax.random.fold_in(key, 2), count)[rank].astype(jnp.int32)


def noise(own_key, shape, width, most, shards=(), kind=jnp.bfloat16):
    array = jax.random.normal(own_key, shape, jnp.float32) * width
    if len(shards) > 0:
        array = block_levels(own_key, shape, shards, -0.22, 0.18) * array
    return jnp.clip(array, min=-most, max=most).astype(kind)


def setup_inputs(seed: int = 0) -> dict:
    keys = jax.random.split(jax.random.key(seed), 10)
    return {
        "section_input": draw_section_input(jax.random.fold_in(keys[9], 71), 0),
        "positions": draw_positions(jax.random.fold_in(keys[9], 71), 0),
        "attn_gain": jnp.clip(1.0 + 0.18 * jax.random.normal(keys[2], (N_SECTION, D), jnp.float32), 0.099609375, 1.8984375).astype(jnp.bfloat16),
        "w_query": draw_w_query(jax.random.fold_in(keys[9], 71), 0),
        "w_keyval": draw_w_keyval(jax.random.fold_in(keys[9], 71), 0),
        "w_out_proj": noise(keys[5], (N_SECTION, QH * HEAD_DIM, D), (QH * HEAD_DIM) ** -0.5, 0.09375, ((0, 16), (1, 8))),
        "final_gain": jnp.clip(1.0 + 0.18 * jax.random.normal(keys[6], (D,), jnp.float32), 0.099609375, 1.8984375).astype(jnp.bfloat16),
        "w_vocab": draw_w_vocab(jax.random.fold_in(keys[9], 71), 0),
        "targets": set_ends(ranked(keys[8], (TOKENS,), VOCAB, 2), jax.random.fold_in(keys[8], 3), 0, VOCAB - 1).astype(jnp.int32),
    }


NORM_EPSILON = 1e-05
ROPE_THETA = 500000.0

def rms_norm(row_block, gain_row):
    values = row_block.astype(jnp.float32)
    factor = lax.rsqrt(lax.optimization_barrier(jnp.mean(values * values, axis=-1, keepdims=True)) + NORM_EPSILON)
    return (values * factor * gain_row.astype(jnp.float32)).astype(jnp.bfloat16)

def rotary(values, token_pos):
    half_dim = values.shape[-1] // 2
    frequency = ROPE_THETA ** (-jnp.arange(half_dim, dtype=jnp.float32) * 2.0 / values.shape[-1])
    angles = token_pos.astype(jnp.float32)[:, None] * frequency[None, :]
    cosine = jnp.cos(angles)[:, None, :]
    sine_part = jnp.sin(angles)[:, None, :]
    lower_half = values[..., :half_dim]
    upper_half = values[..., half_dim:]
    return jnp.concatenate([lower_half * cosine - upper_half * sine_part, upper_half * cosine + lower_half * sine_part], axis=-1)

def allowed_mask(token_pos):
    token_count = token_pos.shape[0]
    query_pos = jnp.arange(token_count, dtype=jnp.int32)[:, None]
    key_pos = jnp.arange(token_count, dtype=jnp.int32)[None, :]
    return (key_pos <= query_pos) & (key_pos >= query_pos - token_pos[:, None])

def decoder_layer(operands):
    hidden, token_pos, gain_row, query_weight, keyval_weight, output_weight = operands
    token_count = hidden.shape[0]
    normed = rms_norm(hidden, gain_row)
    queries = jnp.dot(normed, query_weight, preferred_element_type=jnp.float32).reshape(token_count, -1, HEAD_DIM)
    keyvals = jnp.dot(normed, keyval_weight.reshape(keyval_weight.shape[0], -1), preferred_element_type=jnp.float32)
    keyvals = keyvals.reshape(token_count, keyval_weight.shape[1], 2 * HEAD_DIM)
    queries = rotary(queries, token_pos).astype(jnp.bfloat16)
    key_rows = rotary(keyvals[..., :HEAD_DIM], token_pos).astype(jnp.bfloat16)
    value_rows = keyvals[..., HEAD_DIM:].astype(jnp.bfloat16)
    group_size = queries.shape[1] // key_rows.shape[1]
    key_heads = jnp.repeat(key_rows, group_size, axis=1).astype(jnp.float32)
    value_heads = jnp.repeat(value_rows, group_size, axis=1).astype(jnp.float32)
    scores = jnp.einsum('qhd,khd->hqk', queries.astype(jnp.float32), key_heads) / math.sqrt(HEAD_DIM)
    allowed = allowed_mask(token_pos)[None]
    scores = jnp.where(allowed, scores, -jnp.inf)
    maxima = lax.optimization_barrier(jnp.max(scores, axis=-1, keepdims=True))
    exps = jnp.where(allowed, jnp.exp(scores - maxima), 0.0)
    weights = (exps / lax.optimization_barrier(jnp.sum(exps, axis=-1, keepdims=True))).astype(jnp.bfloat16)
    context = jnp.einsum('hqk,khd->qhd', weights.astype(jnp.float32), value_heads).astype(jnp.bfloat16)
    mixed = jnp.dot(context.reshape(token_count, -1), output_weight, preferred_element_type=jnp.float32)
    return (hidden.astype(jnp.float32) + mixed).astype(jnp.bfloat16)

def reference(section_input, positions, attn_gain, w_query, w_keyval, w_out_proj, final_gain, w_vocab, targets):
    section_outputs = lax.map(decoder_layer, (section_input, positions, attn_gain, w_query, w_keyval, w_out_proj))
    handed = jnp.concatenate([jnp.zeros_like(section_outputs[:1]), section_outputs[:-1]], axis=0)
    final_rows = rms_norm(section_outputs[-1], final_gain)
    logits = jnp.dot(final_rows, w_vocab, preferred_element_type=jnp.float32)
    maxima = lax.optimization_barrier(jnp.max(logits, axis=-1, keepdims=True))
    exp_total = lax.optimization_barrier(jnp.sum(jnp.exp(logits - maxima), axis=-1))
    picked = jnp.take_along_axis(logits, targets[:, None].astype(jnp.int32), axis=-1)[:, 0]
    logprob = picked - maxima[:, 0] - jnp.log(exp_total)
    return (handed, logprob)
```

```python
import math

import jax
import jax.numpy as jnp
from jax import lax
from jax.experimental import pallas as pl
from jax.experimental.pallas import tpu as pltpu
from jax.sharding import PartitionSpec as P

NORM_EPSILON = 1e-05
ROPE_THETA = 500000.0
BF16 = jnp.bfloat16
F32 = jnp.float32
NZ = 4
ROWS = 32
HALF = 16
WIDTH = 8192
HEAD = 128
HEADS = 4
MB = 128
VL = 256


def tensor_pairs(step):
    out = []
    for x in range(2):
        for z in range(NZ):
            x2, z2 = step(x, z)
            out.append((x * NZ + z, (x2 % 2) * NZ + z2 % NZ))
    return out


TO_X = tensor_pairs(lambda x, z: (x + 1, z))
TO_UP = tensor_pairs(lambda x, z: (x, z + 1))
TO_DOWN = tensor_pairs(lambda x, z: (x, z - 1))


def sec(y, h, c):
    return ((y % 4) * 2 + h % 2) * 2 + c


SWAP_CORE = [(s, s ^ 1) for s in range(16)]


def over_tensor(block, pairs):
    return lax.ppermute(block, "tensor", pairs)


def over_section(block, pairs):
    return lax.ppermute(block, "section", pairs)


def rms_norm(row_block, gain_row):
    values = row_block.astype(F32)
    factor = lax.rsqrt(jnp.mean(values * values, axis=-1, keepdims=True) + NORM_EPSILON)
    return (values * factor * gain_row.astype(F32)).astype(BF16)


def gather_rows(own):
    half = own.shape[0] // 2
    from_x = over_tensor(own, TO_X)
    below = over_tensor(own, TO_UP)
    above = over_tensor(own, TO_DOWN)
    x_below = over_tensor(from_x, TO_UP)
    x_above = over_tensor(from_x, TO_DOWN)
    far_a = over_tensor(below[:half], TO_UP)
    far_b = over_tensor(above[half:], TO_DOWN)
    x_far_a = over_tensor(far_a, TO_X)
    x_far_b = over_tensor(far_b, TO_X)
    return own, above, far_a, far_b, below, from_x, x_above, x_far_a, x_far_b, x_below


LAYER_ROWS = [(0, 32), (32, 32), (64, 16), (80, 16), (96, 32), (128, 32), (160, 32), (192, 16), (208, 16), (224, 32)]
KC = 1024
NC = 1024


def layer_kernel(*refs):
    blocks = refs[:10]
    wq_ref, wkv_ref, wo_ref, cos_ref, sin_ref, allow_ref = refs[10:16]
    outs = refs[16:26]
    rows, wq, wkv, wo, q_acc, kv_acc, ctx, res, row_sem, w_sem, wo_sem, out_sem = refs[26:]
    steps = WIDTH // KC

    def row_copies(k):
        cols = pl.ds(k * KC, KC)
        return [
            pltpu.make_async_copy(b.at[:, cols], rows.at[pl.ds(at, n), cols], row_sem.at[k])
            for b, (at, n) in zip(blocks, LAYER_ROWS)
        ]

    def w_copies(k):
        part = pl.ds(k * KC, KC)
        return [
            pltpu.make_async_copy(wq_ref.at[part], wq.at[part], w_sem.at[0, k]),
            pltpu.make_async_copy(wkv_ref.at[part], wkv.at[part], w_sem.at[1, k]),
        ]

    def wo_copy(n):
        cols = pl.ds(n * NC, NC)
        return pltpu.make_async_copy(wo_ref.at[:, cols], wo.at[:, cols], wo_sem.at[n])

    for k in range(steps):
        for c in row_copies(k) + w_copies(k):
            c.start()
    for n in range(WIDTH // NC):
        wo_copy(n).start()
    for k in range(steps):
        cols = pl.ds(k * KC, KC)
        pltpu.make_async_copy(rows.at[:, cols], rows.at[:, cols], row_sem.at[k]).wait()
        for c in w_copies(k):
            c.wait()
        lhs = rows[:, cols]
        q_part = jnp.dot(lhs, wq[cols, :], preferred_element_type=F32)
        kv_part = jnp.dot(lhs, wkv[cols, :], preferred_element_type=F32)
        if k == 0:
            q_acc[...] = q_part
            kv_acc[...] = kv_part
        else:
            q_acc[...] += q_part
            kv_acc[...] += kv_part
    cos, sin = cos_ref[...], sin_ref[...]

    def rotate(v):
        return (v * cos + pltpu.roll(v, HEAD // 2, 1) * sin).astype(BF16)

    keys = rotate(kv_acc[:, :HEAD])
    values = kv_acc[:, HEAD:].astype(BF16)
    for h in range(HEADS):
        q = rotate(q_acc[:, h * HEAD : (h + 1) * HEAD])
        for b in range(2):
            at = slice(b * MB, (b + 1) * MB)
            allow = allow_ref[at, :] > 0
            s = lax.dot_general(q[at], keys[at], (((1,), (1,)), ((), ())), preferred_element_type=F32)
            s = jnp.where(allow, s * (1.0 / math.sqrt(HEAD)), -jnp.inf)
            e = jnp.exp(s - jnp.max(s, axis=1, keepdims=True))
            w = (e / jnp.sum(e, axis=1, keepdims=True)).astype(BF16)
            c = jnp.dot(w, values[at], preferred_element_type=F32)
            ctx[at, h * HEAD : (h + 1) * HEAD] = c.astype(BF16)

    def out_copies(n):
        cols = pl.ds(n * NC, NC)
        return [
            pltpu.make_async_copy(res.at[pl.ds(at, m), cols], o.at[:, cols], out_sem.at[n])
            for o, (at, m) in zip(outs, LAYER_ROWS)
        ]

    for n in range(WIDTH // NC):
        cols = pl.ds(n * NC, NC)
        wo_copy(n).wait()
        res[:, cols] = jnp.dot(ctx[...], wo[:, cols], preferred_element_type=F32).astype(BF16)
        for c in out_copies(n):
            c.start()
    for n in range(WIDTH // NC):
        cols = pl.ds(n * NC, NC)
        pltpu.make_async_copy(res.at[:, cols], res.at[:, cols], out_sem.at[n]).wait()


def layer(blocks, wq, wkv, wo, cos, sin, allow):
    steps = WIDTH // KC
    hbm = pl.BlockSpec(memory_space=pl.ANY)
    vmem = pl.BlockSpec(memory_space=pltpu.VMEM)
    return pl.pallas_call(
        layer_kernel,
        out_shape=[jax.ShapeDtypeStruct((n, WIDTH), BF16) for _, n in LAYER_ROWS],
        in_specs=[hbm] * 13 + [vmem] * 3,
        out_specs=[hbm] * 10,
        scratch_shapes=[
            pltpu.VMEM((2 * MB, WIDTH), BF16),
            pltpu.VMEM((WIDTH, HEADS * HEAD), BF16),
            pltpu.VMEM((WIDTH, 2 * HEAD), BF16),
            pltpu.VMEM((HEADS * HEAD, WIDTH), BF16),
            pltpu.VMEM((2 * MB, HEADS * HEAD), F32),
            pltpu.VMEM((2 * MB, 2 * HEAD), F32),
            pltpu.VMEM((2 * MB, HEADS * HEAD), BF16),
            pltpu.VMEM((2 * MB, WIDTH), BF16),
            pltpu.SemaphoreType.DMA((steps,)),
            pltpu.SemaphoreType.DMA((2, steps)),
            pltpu.SemaphoreType.DMA((WIDTH // NC,)),
            pltpu.SemaphoreType.DMA((WIDTH // NC,)),
        ],
        compiler_params=pltpu.CompilerParams(vmem_limit_bytes=48 * 1024 * 1024),
        cost_estimate=pl.CostEstimate(flops=6 * 10**9, bytes_accessed=28 * 2**20, transcendentals=0),
        name="layer",
    )(*blocks, wq, wkv, wo, cos, sin, allow)


HALF_ROWS = [(0, 16), (16, 16), (32, 8), (40, 8), (48, 16), (64, 16), (80, 16), (96, 8), (104, 8), (112, 16)]
VC = 1024


def vocab_kernel(*refs):
    blocks = refs[:8]
    w0_ref, w1_ref, want_ref, out_ref, rows, w, acc, row_sem, w_sem = refs[8:]
    steps = WIDTH // VC

    def row_copies(k):
        cols = pl.ds(k * VC, VC)
        return [
            pltpu.make_async_copy(b.at[:, cols], rows.at[pl.ds(i * HALF, HALF), cols], row_sem.at[k])
            for i, b in enumerate(blocks)
        ]

    def w_copies(k):
        part = pl.ds(k * VC, VC)
        return [
            pltpu.make_async_copy(r.at[part], w.at[part, pl.ds(i * VL, VL)], w_sem.at[i, k])
            for i, r in enumerate((w0_ref, w1_ref))
        ]

    for k in range(steps):
        for c in row_copies(k) + w_copies(k):
            c.start()
    for k in range(steps):
        cols = pl.ds(k * VC, VC)
        pltpu.make_async_copy(rows.at[:, cols], rows.at[:, cols], row_sem.at[k]).wait()
        for c in w_copies(k):
            c.wait()
        part = jnp.dot(rows[:, cols], w[cols, :], preferred_element_type=F32)
        if k == 0:
            acc[...] = part
        else:
            acc[...] += part
    logits = acc[...]
    top = jnp.max(logits, axis=1, keepdims=True)
    total = jnp.sum(jnp.exp(logits - top), axis=1, keepdims=True)
    column = lax.broadcasted_iota(jnp.int32, logits.shape, 1)
    picked = jnp.sum(jnp.where(column == want_ref[:, :1], logits, 0.0), axis=1, keepdims=True)
    lane = lax.broadcasted_iota(jnp.int32, (8 * HALF, 128), 1)
    out_ref[...] = jnp.where(lane == 0, top, jnp.where(lane == 1, total, picked))


def vocab(blocks, w0, w1, want):
    steps = WIDTH // VC
    hbm = pl.BlockSpec(memory_space=pl.ANY)
    vmem = pl.BlockSpec(memory_space=pltpu.VMEM)
    return pl.pallas_call(
        vocab_kernel,
        out_shape=jax.ShapeDtypeStruct((8 * HALF, 128), F32),
        in_specs=[hbm] * 10 + [vmem],
        out_specs=vmem,
        scratch_shapes=[
            pltpu.VMEM((8 * HALF, WIDTH), BF16),
            pltpu.VMEM((WIDTH, 2 * VL), BF16),
            pltpu.VMEM((8 * HALF, 2 * VL), F32),
            pltpu.SemaphoreType.DMA((steps,)),
            pltpu.SemaphoreType.DMA((2, steps)),
        ],
        compiler_params=pltpu.CompilerParams(vmem_limit_bytes=24 * 1024 * 1024),
        cost_estimate=pl.CostEstimate(flops=10**9, bytes_accessed=10 * 2**20, transcendentals=0),
        name="vocab",
    )(*blocks, w0, w1, want)


def add(*terms):
    return sum(t.astype(F32) for t in terms)


def spread_from_last(final_rows, section, core):
    first = over_section(final_rows[:HALF], [(15, 14)])
    cur = jnp.where(section == 14, first, final_rows[HALF:])
    y, h = section // 4, (section // 2) % 2

    def hop(block, moves):
        return over_section(
            block, [(sec(*a, c), sec(*b, c)) for a, b in moves for c in range(2)]
        )

    up = hop(cur, [((3, 1), (0, 1))])
    down = hop(cur, [((3, 1), (2, 1))])
    side = hop(cur, [((3, 1), (3, 0))])
    got = jnp.where(y == 0, up, jnp.where(y == 2, down, jnp.where(h == 0, side, cur)))
    up = hop(got, [((0, 1), (1, 1))])
    side = hop(got, [((0, 1), (0, 0)), ((2, 1), (2, 0))])
    got = jnp.where(y == 1, up, jnp.where((h == 0) & (y != 3), side, got))
    side = hop(got, [((1, 1), (1, 0))])
    return jnp.where((y == 1) & (h == 0), side, got)


def body(
    section_input, positions, attn_gain, w_query, w_keyval, w_out_proj, final_gain, w_vocab, targets
):
    section, rank = lax.axis_index("section"), lax.axis_index("tensor")
    core, x, z = section % 2, rank // NZ, rank % NZ
    my_rows = section_input[0]
    normed = rms_norm(my_rows, attn_gain[0])
    blocks = gather_rows(normed)
    other_vocab = over_section(w_vocab, SWAP_CORE)

    xs = jnp.stack([x, 1 - x])
    zs = (z + jnp.arange(NZ)) % NZ
    order = (xs[:, None] * NZ + zs[None, :]).reshape(-1)
    place = ((zs * ROWS)[:, None] + jnp.arange(ROWS)[None, :]).reshape(-1)
    pos = jnp.take(positions[0].reshape(8, ROWS), order, axis=0).reshape(-1)
    place2 = jnp.concatenate([place, place])
    frequency = ROPE_THETA ** (-jnp.arange(HEAD // 2, dtype=F32) * 2.0 / HEAD)
    angles = pos.astype(F32)[:, None] * frequency[None, :]
    cos, sin = jnp.cos(angles), jnp.sin(angles)
    cos = jnp.concatenate([cos, cos], axis=1)
    sin = jnp.concatenate([-sin, sin], axis=1)
    keys_at = place[None, :]
    allow = ((keys_at <= place2[:, None]) & (keys_at >= (place2 - pos)[:, None])).astype(F32)

    parts = layer(
        blocks, w_query[0], w_keyval[0].reshape(WIDTH, -1), w_out_proj[0], cos, sin, allow
    )
    own, above, far_a, far_b, below, x_own, x_above, x_far_a, x_far_b, x_below = parts
    got_far_a = over_tensor(x_far_a, TO_X)
    got_far_b = over_tensor(x_far_b, TO_X)
    got_x_down = over_tensor(x_above, TO_UP)
    got_x_up = over_tensor(x_below, TO_DOWN)
    far_a = add(far_a, got_far_a).astype(BF16)
    far_b = add(far_b, got_far_b).astype(BF16)
    got_a = over_tensor(far_a, TO_DOWN)
    got_b = over_tensor(far_b, TO_UP)
    x_own = add(x_own, got_x_down, got_x_up).astype(BF16)
    got_x = over_tensor(x_own, TO_X)
    below = jnp.concatenate([add(below[:HALF], got_a), below[HALF:].astype(F32)], axis=0).astype(BF16)
    above = jnp.concatenate([above[:HALF].astype(F32), add(above[HALF:], got_b)], axis=0).astype(BF16)
    got_down = over_tensor(below, TO_DOWN)
    got_up = over_tensor(above, TO_UP)
    layer_out = add(my_rows, own, got_x, got_down, got_up).astype(BF16)

    final_rows = rms_norm(layer_out, final_gain)
    mine = spread_from_last(final_rows, section, core)
    handed = over_section(layer_out, [(s, s + 1) for s in range(15)])[None]

    b = gather_rows(mine)
    blocks = (
        b[0], b[1], jnp.concatenate([b[2], b[3]]), b[4],
        b[5], b[6], jnp.concatenate([b[7], b[8]]), b[9],
    )
    starts = jnp.stack([section, section ^ 1]) * 8 * VL + rank * VL
    mine_targets = jnp.take(targets.reshape(8, 2, HALF), core, axis=1)
    want = jnp.take(mine_targets, order, axis=0).reshape(-1)
    at = want[:, None] - starts[None, :]
    inside = (at >= 0) & (at < VL)
    want = jnp.max(jnp.where(inside, at + jnp.arange(2)[None, :] * VL, -1), axis=1)
    want = jnp.broadcast_to(want[:, None], (8 * HALF, 128))
    stats = vocab(blocks, w_vocab, other_vocab, want)[:, :3]
    rank_x, rank_z = jnp.arange(8) // NZ, jnp.arange(8) % NZ
    seen_at = (rank_x ^ x) * NZ + (rank_z - z) % NZ
    stats = jnp.take(stats.reshape(8, HALF * 3), seen_at, axis=0)
    sent = jnp.broadcast_to(stats[None], (16, 8, HALF * 3)).reshape(128, HALF * 3)
    got = lax.all_to_all(sent, ("section", "tensor"), 0, 0, tiled=True)
    got = got.reshape(8, 2, 8, HALF, 3)
    tops, totals, picks = got[..., 0], got[..., 1], got[..., 2]
    top = jnp.max(tops, axis=(0, 2))
    total = jnp.sum(totals * jnp.exp(tops - top[None, :, None, :]), axis=(0, 2))
    logprob = jnp.sum(picks, axis=(0, 2)) - top - jnp.log(total)
    return handed, logprob.reshape(-1)


def solution(mesh):
    placed = (
        P("section", "tensor", None),
        P("section", None),
        P("section", None),
        P("section", None, "tensor"),
        P("section", None, "tensor", None),
        P("section", "tensor", None),
        P(),
        P(None, ("section", "tensor")),
        P(),
    )
    return jax.shard_map(
        body,
        mesh=mesh,
        in_specs=placed,
        out_specs=(P("section", "tensor", None), P("tensor")),
        check_vma=False,
    )
```

```python
import math

import jax
import jax.numpy as jnp
from jax import lax
from jax.experimental import pallas as pl
from jax.experimental.pallas import tpu as pltpu
from jax.sharding import PartitionSpec as P

NORM_EPSILON = 1e-05
ROPE_THETA = 500000.0
BF16 = jnp.bfloat16
F32 = jnp.float32
NZ = 4
ROWS = 32
HALF = 16
WIDTH = 8192
HEAD = 128
HEADS = 4
MB = 128
VL = 256


def tensor_pairs(step):
    out = []
    for x in range(2):
        for z in range(NZ):
            x2, z2 = step(x, z)
            out.append((x * NZ + z, (x2 % 2) * NZ + z2 % NZ))
    return out


TO_X = tensor_pairs(lambda x, z: (x + 1, z))
TO_UP = tensor_pairs(lambda x, z: (x, z + 1))
TO_DOWN = tensor_pairs(lambda x, z: (x, z - 1))


def sec(y, h, c):
    return ((y % 4) * 2 + h % 2) * 2 + c


def over_tensor(block, pairs):
    return lax.ppermute(block, "tensor", pairs)


def over_section(block, pairs):
    return lax.ppermute(block, "section", pairs)


def rms_norm(row_block, gain_row):
    values = row_block.astype(F32)
    factor = lax.rsqrt(jnp.mean(values * values, axis=-1, keepdims=True) + NORM_EPSILON)
    return (values * factor * gain_row.astype(F32)).astype(BF16)


def gather_rows(own):
    half = own.shape[0] // 2

    def move(block, pairs):
        return over_tensor(block, pairs)

    from_x = move(own, TO_X)
    below = move(own, TO_UP)
    above = move(own, TO_DOWN)
    far_a = move(below[:half], TO_UP)
    far_b = move(above[half:], TO_DOWN)
    x_below = move(from_x, TO_UP)
    x_above = move(from_x, TO_DOWN)
    x_far_a = move(far_a, TO_X)
    x_far_b = move(far_b, TO_X)
    return own, above, far_a, far_b, below, from_x, x_above, x_far_a, x_far_b, x_below


def scatter_sum(parts, my_rows):
    def move(block, pairs):
        return over_tensor(block, pairs)

    own, above, far_a, far_b, below, x_own, x_above, x_far_a, x_far_b, x_below = parts
    got_far_a = move(x_far_a, TO_X)
    got_far_b = move(x_far_b, TO_X)
    got_x_down = move(x_above, TO_UP)
    got_x_up = move(x_below, TO_DOWN)
    far_a = add(far_a, got_far_a).astype(BF16)
    far_b = add(far_b, got_far_b).astype(BF16)
    got_a = move(far_a, TO_DOWN)
    got_b = move(far_b, TO_UP)
    x_own = add(x_own, got_x_down, got_x_up).astype(BF16)
    got_x = move(x_own, TO_X)
    below = jnp.concatenate([add(below[:HALF], got_a), below[HALF:].astype(F32)], axis=0).astype(BF16)
    above = jnp.concatenate([above[:HALF].astype(F32), add(above[HALF:], got_b)], axis=0).astype(BF16)
    got_down = move(below, TO_DOWN)
    got_up = move(above, TO_UP)
    return add(my_rows, own, got_x, got_down, got_up).astype(BF16)


LAYER_ROWS = [(0, 32), (32, 32), (64, 16), (80, 16), (96, 32), (128, 32), (160, 32), (192, 16), (208, 16), (224, 32)]
KC = 2048
NC = 2048
QKV = (HEADS + 2) * HEAD


def at(k, size):
    return pl.ds(pl.multiple_of(k * size, size), size)


def layer_kernel(*refs):
    blocks = refs[:10]
    wq_ref, wkv_ref, wo_ref, cos_ref, sin_ref, allow_ref = refs[10:16]
    outs = refs[16:26]
    rows, w, wo, acc, ctx, res, row_sem, w_sem, wo_sem, out_sem = refs[26:]

    for b, (r, n) in zip(blocks, LAYER_ROWS):
        pltpu.make_async_copy(b, rows.at[pl.ds(r, n)], row_sem).start()

    @pl.loop(0, WIDTH // KC)
    def _(k):
        cols = at(k, KC)
        q_cols, kv_cols = pl.ds(0, HEADS * HEAD), pl.ds(HEADS * HEAD, 2 * HEAD)
        pltpu.make_async_copy(wq_ref.at[cols], w.at[cols, q_cols], w_sem.at[k]).start()
        pltpu.make_async_copy(wkv_ref.at[cols], w.at[cols, kv_cols], w_sem.at[k]).start()

    @pl.loop(0, WIDTH // NC)
    def _(n):
        cols = at(n, NC)
        pltpu.make_async_copy(wo_ref.at[:, cols], wo.at[:, cols], wo_sem.at[n]).start()

    acc[...] = jnp.zeros_like(acc)
    pltpu.make_async_copy(rows, rows, row_sem).wait()

    @pl.loop(0, WIDTH // KC)
    def _(k):
        cols = at(k, KC)
        pltpu.make_async_copy(w.at[cols], w.at[cols], w_sem.at[k]).wait()
        acc[...] += jnp.dot(rows[:, cols], w[cols, :], preferred_element_type=F32)

    cos, sin = cos_ref[...], sin_ref[...]

    def rotated(h):
        v = acc[:, h * HEAD : (h + 1) * HEAD]
        return (v * cos + pltpu.roll(v, HEAD // 2, 1) * sin).astype(BF16)

    keys = rotated(HEADS)
    values = acc[:, (HEADS + 1) * HEAD :].astype(BF16)
    heads = [rotated(h) for h in range(HEADS)]
    for b in range(2):
        mb = slice(b * MB, (b + 1) * MB)
        allow = jnp.concatenate([allow_ref[mb, :]] * HEADS, axis=0) > 0
        q = jnp.concatenate([head[mb] for head in heads], axis=0)
        s = lax.dot_general(q, keys[mb], (((1,), (1,)), ((), ())), preferred_element_type=F32)
        s = jnp.where(allow, s * (1.0 / math.sqrt(HEAD)), -jnp.inf)
        e = jnp.exp(s - jnp.max(s, axis=1, keepdims=True))
        p = (e / jnp.sum(e, axis=1, keepdims=True)).astype(BF16)
        c = jnp.dot(p, values[mb], preferred_element_type=F32).astype(BF16)
        for h in range(HEADS):
            ctx[mb, h * HEAD : (h + 1) * HEAD] = c[h * MB : (h + 1) * MB]

    @pl.loop(0, WIDTH // NC)
    def _(n):
        cols = at(n, NC)
        pltpu.make_async_copy(wo.at[:, cols], wo.at[:, cols], wo_sem.at[n]).wait()
        res[:, cols] = jnp.dot(ctx[...], wo[:, cols], preferred_element_type=F32).astype(BF16)
        for o, (r, m) in zip(outs, LAYER_ROWS):
            pltpu.make_async_copy(res.at[pl.ds(r, m), cols], o.at[:, cols], out_sem).start()

    pltpu.make_async_copy(res, res, out_sem).wait()


def layer(blocks, wq, wkv, wo, cos, sin, allow):
    hbm = pl.BlockSpec(memory_space=pl.ANY)
    vmem = pl.BlockSpec(memory_space=pltpu.VMEM)
    return pl.pallas_call(
        layer_kernel,
        out_shape=[jax.ShapeDtypeStruct((n, WIDTH), BF16) for _, n in LAYER_ROWS],
        in_specs=[hbm] * 13 + [vmem] * 3,
        out_specs=[hbm] * 10,
        scratch_shapes=[
            pltpu.VMEM((2 * MB, WIDTH), BF16),
            pltpu.VMEM((WIDTH, QKV), BF16),
            pltpu.VMEM((HEADS * HEAD, WIDTH), BF16),
            pltpu.VMEM((2 * MB, QKV), F32),
            pltpu.VMEM((2 * MB, HEADS * HEAD), BF16),
            pltpu.VMEM((2 * MB, WIDTH), BF16),
            pltpu.SemaphoreType.DMA,
            pltpu.SemaphoreType.DMA((WIDTH // KC,)),
            pltpu.SemaphoreType.DMA((WIDTH // NC,)),
            pltpu.SemaphoreType.DMA,
        ],
        compiler_params=pltpu.CompilerParams(vmem_limit_bytes=48 * 1024 * 1024),
        cost_estimate=pl.CostEstimate(flops=6 * 10**9, bytes_accessed=28 * 2**20, transcendentals=0),
        name="layer",
    )(*blocks, wq, wkv, wo, cos, sin, allow)


VC = 2048


def vocab_kernel(*refs):
    blocks = refs[:10]
    w0_ref, w1_ref, want_ref, out_ref, rows, w, acc, row_sem, w_sem = refs[10:]

    for b, (r, n) in zip(blocks, LAYER_ROWS):
        pltpu.make_async_copy(b, rows.at[pl.ds(r, n)], row_sem).start()

    @pl.loop(0, WIDTH // VC, unroll=True)
    def _(k):
        cols = at(k, VC)
        for i, r in enumerate((w0_ref, w1_ref)):
            pltpu.make_async_copy(r.at[cols], w.at[cols, pl.ds(i * VL, VL)], w_sem.at[k]).start()

    acc[...] = jnp.zeros_like(acc)
    pltpu.make_async_copy(rows, rows, row_sem).wait()

    @pl.loop(0, WIDTH // VC, unroll=True)
    def _(k):
        cols = at(k, VC)
        pltpu.make_async_copy(w.at[cols], w.at[cols], w_sem.at[k]).wait()
        acc[...] += jnp.dot(rows[:, cols], w[cols, :], preferred_element_type=F32)

    logits = acc[...]
    top = jnp.max(logits, axis=1, keepdims=True)
    total = jnp.sum(jnp.exp(logits - top), axis=1, keepdims=True)
    column = lax.broadcasted_iota(jnp.int32, logits.shape, 1)
    picked = jnp.sum(jnp.where(column == want_ref[:, :1], logits, 0.0), axis=1, keepdims=True)
    lane = lax.broadcasted_iota(jnp.int32, (2 * MB, 128), 1)
    out_ref[...] = jnp.where(lane == 0, top, jnp.where(lane == 1, total, picked))


def vocab(blocks, w0, w1, want):
    hbm = pl.BlockSpec(memory_space=pl.ANY)
    vmem = pl.BlockSpec(memory_space=pltpu.VMEM)
    return pl.pallas_call(
        vocab_kernel,
        out_shape=jax.ShapeDtypeStruct((2 * MB, 128), F32),
        in_specs=[hbm] * 12 + [vmem],
        out_specs=vmem,
        scratch_shapes=[
            pltpu.VMEM((2 * MB, WIDTH), BF16),
            pltpu.VMEM((WIDTH, 2 * VL), BF16),
            pltpu.VMEM((2 * MB, 2 * VL), F32),
            pltpu.SemaphoreType.DMA,
            pltpu.SemaphoreType.DMA((WIDTH // VC,)),
        ],
        compiler_params=pltpu.CompilerParams(vmem_limit_bytes=48 * 1024 * 1024),
        cost_estimate=pl.CostEstimate(flops=2 * 10**9, bytes_accessed=14 * 2**20, transcendentals=0),
        name="vocab",
    )(*blocks, w0, w1, want)


def add(*terms):
    return sum(t.astype(F32) for t in terms)


def spread_from_last(final_rows, section):
    y = section // 4

    def hop(block, moves):
        return over_section(block, [(sec(*a, 1), sec(*b, 1)) for a, b in moves])

    side = hop(final_rows, [((3, 1), (3, 0))])
    rows = jnp.where(section == 15, final_rows, side)
    up = hop(rows, [((3, h), (0, h)) for h in range(2)])
    down = hop(rows, [((3, h), (2, h)) for h in range(2)])
    across = hop(rows, [((3, h), (1, h)) for h in range(2)])
    return jnp.where(y == 3, rows, jnp.where(y == 0, up, jnp.where(y == 2, down, across)))


def body(
    section_input, positions, attn_gain, w_query, w_keyval, w_out_proj, final_gain, w_vocab, targets
):
    section, rank = lax.axis_index("section"), lax.axis_index("tensor")
    core, x, z = section % 2, rank // NZ, rank % NZ
    my_rows = section_input[0]
    normed = rms_norm(my_rows, attn_gain[0])
    other_vocab = over_section(w_vocab, [(s, s + 1) for s in range(0, 16, 2)])
    xs = jnp.stack([x, 1 - x])
    zs = (z + jnp.arange(NZ)) % NZ
    order = (xs[:, None] * NZ + zs[None, :]).reshape(-1)

    def tables():
        place = ((zs * ROWS)[:, None] + jnp.arange(ROWS)[None, :]).reshape(-1)
        pos = jnp.take(positions[0].reshape(8, ROWS), order, axis=0).reshape(-1)
        place2 = jnp.concatenate([place, place])
        frequency = ROPE_THETA ** (-jnp.arange(HEAD // 2, dtype=F32) * 2.0 / HEAD)
        angles = pos.astype(F32)[:, None] * frequency[None, :]
        cos, sin = jnp.cos(angles), jnp.sin(angles)
        cos = jnp.concatenate([cos, cos], axis=1)
        sin = jnp.concatenate([-sin, sin], axis=1)
        keys_at = place[None, :]
        allow = ((keys_at <= place2[:, None]) & (keys_at >= (place2 - pos)[:, None])).astype(F32)

        starts = jnp.stack([section, section ^ 1]) * 8 * VL + rank * VL
        want = jnp.take(targets.reshape(8, ROWS), order, axis=0).reshape(-1)
        local = want[:, None] - starts[None, :]
        inside = (local >= 0) & (local < VL)
        want = jnp.max(jnp.where(inside, local + jnp.arange(2)[None, :] * VL, -1), axis=1)
        want = jnp.broadcast_to(want[:, None], (2 * MB, 128))
        return cos, sin, allow, want

    odd_blocks, mark, (cos, sin, allow, want) = lax.cond(
        core == 1,
        lambda rows: (gather_rows(rows)[1:], rows[:HALF, :HEAD], tables()),
        lambda rows: (
            tuple(jnp.zeros((n, WIDTH), BF16) for _, n in LAYER_ROWS[1:]),
            rows[:HALF, :HEAD],
            tables(),
        ),
        normed,
    )
    token = over_section(mark, [(s, s - 1) for s in range(1, 16, 2)])
    weights = (w_query[0], w_keyval[0].reshape(WIDTH, -1), w_out_proj[0], cos, sin, allow)

    def odd_path():
        parts = layer((normed, *odd_blocks), *weights)
        layer_out = scatter_sum(parts, my_rows)
        mine = spread_from_last(rms_norm(layer_out, final_gain), section)
        stats = vocab(gather_rows(mine), w_vocab, other_vocab, want)
        return layer_out, stats[:, :3]

    def even_path():
        later = jnp.where(token[0, 0] > 1e4, jnp.zeros_like(normed), normed)
        parts = layer(gather_rows(later), *weights)
        return scatter_sum(parts, my_rows), jnp.zeros((2 * MB, 3), F32)

    layer_out, stats = lax.cond(core == 1, odd_path, even_path)
    handed = over_section(layer_out, [(s, s + 1) for s in range(15)])[None]
    rank_x, rank_z = jnp.arange(8) // NZ, jnp.arange(8) % NZ
    seen_at = (rank_x ^ x) * NZ + (rank_z - z) % NZ
    stats = jnp.take(stats.reshape(8, ROWS * 3), seen_at, axis=0)
    sent = jnp.broadcast_to(stats[None], (16, 8, ROWS * 3)).reshape(128, ROWS * 3)
    got = lax.all_to_all(sent, ("section", "tensor"), 0, 0, tiled=True)
    got = got.reshape(8, 2, 8, ROWS, 3)[:, 1]
    tops, totals, picks = got[..., 0], got[..., 1], got[..., 2]
    top = jnp.max(tops, axis=(0, 1))
    total = jnp.sum(totals * jnp.exp(tops - top), axis=(0, 1))
    logprob = jnp.sum(picks, axis=(0, 1)) - top - jnp.log(total)
    return handed, logprob


def solution(mesh):
    placed = (
        P("section", "tensor", None),
        P("section", None),
        P("section", None),
        P("section", None, "tensor"),
        P("section", None, "tensor", None),
        P("section", "tensor", None),
        P(),
        P(None, ("section", "tensor")),
        P(),
    )
    return jax.shard_map(
        body,
        mesh=mesh,
        in_specs=placed,
        out_specs=(P("section", "tensor", None), P("tensor")),
        check_vma=False,
    )
```

```python
import math

import jax
import jax.numpy as jnp
from jax import lax
from jax.experimental import pallas as pl
from jax.experimental.pallas import tpu as pltpu
from jax.sharding import PartitionSpec as P

NORM_EPSILON = 1e-05
ROPE_THETA = 500000.0
BF16 = jnp.bfloat16
F32 = jnp.float32
NZ = 4
ROWS = 32
HALF = 16
WIDTH = 8192
HEAD = 128
HEADS = 4
MB = 128
VL = 256


def tensor_pairs(step):
    out = []
    for x in range(2):
        for z in range(NZ):
            x2, z2 = step(x, z)
            out.append((x * NZ + z, (x2 % 2) * NZ + z2 % NZ))
    return out


TO_X = tensor_pairs(lambda x, z: (x + 1, z))
TO_UP = tensor_pairs(lambda x, z: (x, z + 1))
TO_DOWN = tensor_pairs(lambda x, z: (x, z - 1))


def sec(y, h, c):
    return ((y % 4) * 2 + h % 2) * 2 + c


def over_tensor(block, pairs):
    return lax.ppermute(block, "tensor", pairs)


def over_section(block, pairs):
    return lax.ppermute(block, "section", pairs)


def gather_first(own):
    from_x = over_tensor(own, TO_X)
    below = over_tensor(own, TO_UP)
    above = over_tensor(own, TO_DOWN)
    return above, over_tensor(below, TO_UP), below, from_x


def gather_rest(own, first):
    above, far, below, from_x = first
    x_far = over_tensor(far, TO_X)
    x_below = over_tensor(from_x, TO_UP)
    x_above = over_tensor(from_x, TO_DOWN)
    return own, above, far, below, from_x, x_above, x_far, x_below


def gather_rows(own):
    return gather_rest(own, gather_first(own))


def scatter_sum(parts):
    own, above, far, below, x_own, x_above, x_far, x_below = parts
    got_far = over_tensor(x_far, TO_X)
    got_x_down = over_tensor(x_above, TO_UP)
    got_x_up = over_tensor(x_below, TO_DOWN)
    far_a = add(far[:HALF], got_far[:HALF]).astype(BF16)
    far_b = add(far[HALF:], got_far[HALF:]).astype(BF16)
    got_a = over_tensor(far_a, TO_DOWN)
    got_b = over_tensor(far_b, TO_UP)
    x_own = add(x_own, got_x_down, got_x_up).astype(BF16)
    got_x = over_tensor(x_own, TO_X)
    below = jnp.concatenate([add(below[:HALF], got_a), below[HALF:].astype(F32)], axis=0).astype(BF16)
    above = jnp.concatenate([above[:HALF].astype(F32), add(above[HALF:], got_b)], axis=0).astype(BF16)
    got_down = over_tensor(below, TO_DOWN)
    got_up = over_tensor(above, TO_UP)
    return own, got_x, got_down, got_up


def norm_value(values, gain):
    factor = lax.rsqrt(jnp.mean(values * values, axis=-1, keepdims=True) + NORM_EPSILON)
    return (values * factor * gain.astype(F32)).astype(BF16)


def norm_kernel(rows_ref, gain_ref, out_ref):
    out_ref[...] = norm_value(rows_ref[...].astype(F32), gain_ref[...])


def rms_norm(rows, gain):
    return pl.pallas_call(
        norm_kernel, out_shape=jax.ShapeDtypeStruct(rows.shape, BF16), name="norm"
    )(rows, gain.reshape(1, -1))


def finish_kernel(rows_ref, a_ref, b_ref, c_ref, d_ref, gain_ref, out_ref, final_ref):
    out = add(rows_ref[...], a_ref[...], b_ref[...], c_ref[...], d_ref[...]).astype(BF16)
    out_ref[...] = out
    final_ref[...] = norm_value(out.astype(F32), gain_ref[...])


def finish(rows, terms, gain):
    return pl.pallas_call(
        finish_kernel,
        out_shape=[jax.ShapeDtypeStruct(rows.shape, BF16)] * 2,
        compiler_params=pltpu.CompilerParams(vmem_limit_bytes=24 * 1024 * 1024),
        name="finish",
    )(rows, *terms, gain.reshape(1, -1))


def merge_kernel(got_ref, out_ref):
    got = got_ref[...].reshape(8, 2, 8, 128)[:, 1].reshape(64, 128)
    tops, totals, picks = got[:, :ROWS], got[:, ROWS : 2 * ROWS], got[:, 2 * ROWS : 3 * ROWS]
    top = jnp.max(tops, axis=0, keepdims=True)
    total = jnp.sum(totals * jnp.exp(tops - top), axis=0, keepdims=True)
    out_ref[...] = (jnp.sum(picks, axis=0, keepdims=True) - top - jnp.log(total))[0]


def merge(got):
    return pl.pallas_call(
        merge_kernel, out_shape=jax.ShapeDtypeStruct((ROWS,), F32), name="merge"
    )(got)


KC = 2048
NC = 2048
QKV = (HEADS + 2) * HEAD


def at(k, size):
    return pl.ds(pl.multiple_of(k * size, size), size)


def layer_kernel(*refs):
    blocks = refs[:8]
    wq_ref, wkv_ref, wo_ref, cos_ref, sin_ref, allow_ref = refs[8:14]
    outs = refs[14:22]
    rows, w, wo, acc, ctx, res, row_sem, w_sem, wo_sem, out_sem = refs[22:]

    for i, b in enumerate(blocks):
        pltpu.make_async_copy(b, rows.at[pl.ds(i * ROWS, ROWS)], row_sem).start()

    @pl.loop(0, WIDTH // KC)
    def _(k):
        cols = at(k, KC)
        q_cols, kv_cols = pl.ds(0, HEADS * HEAD), pl.ds(HEADS * HEAD, 2 * HEAD)
        pltpu.make_async_copy(wq_ref.at[cols], w.at[cols, q_cols], w_sem.at[k]).start()
        pltpu.make_async_copy(wkv_ref.at[cols], w.at[cols, kv_cols], w_sem.at[k]).start()

    @pl.loop(0, WIDTH // NC)
    def _(n):
        cols = at(n, NC)
        pltpu.make_async_copy(wo_ref.at[:, cols], wo.at[:, cols], wo_sem.at[n]).start()

    acc[...] = jnp.zeros_like(acc)
    pltpu.make_async_copy(rows, rows, row_sem).wait()

    @pl.loop(0, WIDTH // KC)
    def _(k):
        cols = at(k, KC)
        pltpu.make_async_copy(w.at[cols], w.at[cols], w_sem.at[k]).wait()
        acc[...] += jnp.dot(rows[:, cols], w[cols, :], preferred_element_type=F32)

    cos, sin = cos_ref[...], sin_ref[...]

    def rotated(h):
        v = acc[:, h * HEAD : (h + 1) * HEAD]
        return (v * cos + pltpu.roll(v, HEAD // 2, 1) * sin).astype(BF16)

    keys = rotated(HEADS)
    values = acc[:, (HEADS + 1) * HEAD :].astype(BF16)
    heads = [rotated(h) for h in range(HEADS)]
    for b in range(2):
        mb = slice(b * MB, (b + 1) * MB)
        allow = jnp.concatenate([allow_ref[mb, :]] * HEADS, axis=0) > 0
        q = jnp.concatenate([head[mb] for head in heads], axis=0)
        s = lax.dot_general(q, keys[mb], (((1,), (1,)), ((), ())), preferred_element_type=F32)
        s = jnp.where(allow, s * (1.0 / math.sqrt(HEAD)), -jnp.inf)
        e = jnp.exp(s - jnp.max(s, axis=1, keepdims=True))
        p = (e / jnp.sum(e, axis=1, keepdims=True)).astype(BF16)
        c = jnp.dot(p, values[mb], preferred_element_type=F32).astype(BF16)
        for h in range(HEADS):
            ctx[mb, h * HEAD : (h + 1) * HEAD] = c[h * MB : (h + 1) * MB]

    @pl.loop(0, WIDTH // NC)
    def _(n):
        cols = at(n, NC)
        pltpu.make_async_copy(wo.at[:, cols], wo.at[:, cols], wo_sem.at[n]).wait()
        res[:, cols] = jnp.dot(ctx[...], wo[:, cols], preferred_element_type=F32).astype(BF16)
        for i, o in enumerate(outs):
            pltpu.make_async_copy(res.at[pl.ds(i * ROWS, ROWS), cols], o.at[:, cols], out_sem).start()

    pltpu.make_async_copy(res, res, out_sem).wait()


def layer(blocks, wq, wkv, wo, cos, sin, allow):
    hbm = pl.BlockSpec(memory_space=pl.ANY)
    vmem = pl.BlockSpec(memory_space=pltpu.VMEM)
    return pl.pallas_call(
        layer_kernel,
        out_shape=[jax.ShapeDtypeStruct((ROWS, WIDTH), BF16)] * 8,
        in_specs=[hbm] * 11 + [vmem] * 3,
        out_specs=[hbm] * 8,
        scratch_shapes=[
            pltpu.VMEM((2 * MB, WIDTH), BF16),
            pltpu.VMEM((WIDTH, QKV), BF16),
            pltpu.VMEM((HEADS * HEAD, WIDTH), BF16),
            pltpu.VMEM((2 * MB, QKV), F32),
            pltpu.VMEM((2 * MB, HEADS * HEAD), BF16),
            pltpu.VMEM((2 * MB, WIDTH), BF16),
            pltpu.SemaphoreType.DMA,
            pltpu.SemaphoreType.DMA((WIDTH // KC,)),
            pltpu.SemaphoreType.DMA((WIDTH // NC,)),
            pltpu.SemaphoreType.DMA,
        ],
        compiler_params=pltpu.CompilerParams(vmem_limit_bytes=48 * 1024 * 1024),
        cost_estimate=pl.CostEstimate(flops=6 * 10**9, bytes_accessed=28 * 2**20, transcendentals=0),
        name="layer",
    )(*blocks, wq, wkv, wo, cos, sin, allow)


VC = 2048


def vocab_kernel(order_ref, *refs):
    blocks = refs[:8]
    w0_ref, w1_ref, want_ref, out_ref, rows, w, acc, row_sem, w_sem = refs[8:]
    for i, b in enumerate(blocks):
        pltpu.make_async_copy(b, rows.at[pl.ds(i * ROWS, ROWS)], row_sem).start()

    @pl.loop(0, WIDTH // VC)
    def _(k):
        cols = at(k, VC)
        for i, r in enumerate((w0_ref, w1_ref)):
            pltpu.make_async_copy(r.at[cols], w.at[cols, pl.ds(i * VL, VL)], w_sem.at[k]).start()

    acc[...] = jnp.zeros_like(acc)
    pltpu.make_async_copy(rows, rows, row_sem).wait()

    @pl.loop(0, WIDTH // VC, unroll=True)
    def _(k):
        cols = at(k, VC)
        pltpu.make_async_copy(w.at[cols], w.at[cols], w_sem.at[k]).wait()
        acc[...] += jnp.dot(rows[:, cols], w[cols, :], preferred_element_type=F32)

    logits = acc[...]
    top = jnp.max(logits, axis=1, keepdims=True)
    total = jnp.sum(jnp.exp(logits - top), axis=1, keepdims=True)
    column = lax.broadcasted_iota(jnp.int32, logits.shape, 1)
    picked = jnp.sum(jnp.where(column == want_ref[:, :1], logits, 0.0), axis=1, keepdims=True)
    lane = lax.broadcasted_iota(jnp.int32, (2 * MB, 128), 1)
    stats = jnp.where(lane == 0, top, jnp.where(lane == 1, total, picked)).T
    for i in range(8):
        mine = slice(i * ROWS, (i + 1) * ROWS)
        line = jnp.concatenate([stats[k : k + 1, mine] for k in (0, 1, 2, 2)], axis=1)
        out_ref[pl.ds(order_ref[i], 1), :] = line
    lines = out_ref[:8, :]
    for s in range(1, 16):
        out_ref[s * 8 : (s + 1) * 8, :] = lines


def vocab(order, blocks, w0, w1, want):
    hbm = pl.BlockSpec(memory_space=pl.ANY)
    vmem = pl.BlockSpec(memory_space=pltpu.VMEM)
    return pl.pallas_call(
        vocab_kernel,
        out_shape=jax.ShapeDtypeStruct((128, 128), F32),
        in_specs=[pl.BlockSpec(memory_space=pltpu.SMEM)] + [hbm] * 10 + [vmem],
        out_specs=vmem,
        scratch_shapes=[
            pltpu.VMEM((2 * MB, WIDTH), BF16),
            pltpu.VMEM((WIDTH, 2 * VL), BF16),
            pltpu.VMEM((2 * MB, 2 * VL), F32),
            pltpu.SemaphoreType.DMA,
            pltpu.SemaphoreType.DMA((WIDTH // VC,)),
        ],
        compiler_params=pltpu.CompilerParams(vmem_limit_bytes=48 * 1024 * 1024),
        cost_estimate=pl.CostEstimate(flops=2 * 10**9, bytes_accessed=14 * 2**20, transcendentals=0),
        name="vocab",
    )(order, *blocks, w0, w1, want)


def add(*terms):
    return sum(t.astype(F32) for t in terms)


BESIDE = [(r, r ^ (2 * 8) ^ NZ) for r in range(128)]


def spread_from_last(final_rows, section):
    y, h = section // 4, section // 2 % 2

    def hop(to):
        return over_section(final_rows, [(15, sec(to, 1, 1))])

    up, down, across = hop(0), hop(2), hop(1)
    rows = jnp.where(y == 3, final_rows, jnp.where(y == 0, up, jnp.where(y == 2, down, across)))
    here = [(r, to) for r, to in BESIDE if r // 8 % 4 == 3]
    return jnp.where(h == 1, rows, lax.ppermute(rows, ("section", "tensor"), here))


def body(
    section_input, positions, attn_gain, w_query, w_keyval, w_out_proj, final_gain, w_vocab, targets
):
    section, rank = lax.axis_index("section"), lax.axis_index("tensor")
    core, x, z = section % 2, rank // NZ, rank % NZ
    my_rows = section_input[0]
    normed = rms_norm(my_rows, attn_gain[0])
    other_vocab = over_section(w_vocab, [(s, s + 1) for s in range(0, 16, 2)])

    zs = (z + jnp.arange(NZ)) % NZ

    def order_from(first_x):
        return (jnp.stack([first_x, 1 - first_x])[:, None] * NZ + zs[None, :]).reshape(-1)

    def tables():
        place = ((zs * ROWS)[:, None] + jnp.arange(ROWS)[None, :]).reshape(-1)
        pos = jnp.take(positions[0].reshape(8, ROWS), order_from(x), axis=0).reshape(-1)
        place2 = jnp.concatenate([place, place])
        frequency = ROPE_THETA ** (-jnp.arange(HEAD // 2, dtype=F32) * 2.0 / HEAD)
        angles = pos.astype(F32)[:, None] * frequency[None, :]
        cos, sin = jnp.cos(angles), jnp.sin(angles)
        cos = jnp.concatenate([cos, cos], axis=1)
        sin = jnp.concatenate([-sin, sin], axis=1)
        keys_at = place[None, :]
        allow = ((keys_at <= place2[:, None]) & (keys_at >= (place2 - pos)[:, None])).astype(F32)
        return cos, sin, allow

    odd = core == 1
    blank = jnp.zeros((ROWS, WIDTH), BF16)
    weights = (w_query[0], w_keyval[0].reshape(WIDTH, -1), w_out_proj[0])
    blocks, angles = lax.cond(
        odd, lambda: (gather_rows(normed), tables()), lambda: ((blank,) * 8, tables())
    )
    def layer_rows(blocks):
        return finish(my_rows, scatter_sum(layer(blocks, *weights, *angles)), final_gain)

    def odd_path():
        layer_out, final_rows = layer_rows(blocks)
        order = order_from(jnp.where(section // 2 % 2 == 1, x, 1 - x))
        starts = jnp.stack([section, section ^ 1]) * 8 * VL + rank * VL
        want = jnp.take(targets.reshape(8, ROWS), order, axis=0).reshape(-1)
        local = want[:, None] - starts[None, :]
        inside = (local >= 0) & (local < VL)
        want = jnp.max(jnp.where(inside, local + jnp.arange(2)[None, :] * VL, -1), axis=1)
        want = jnp.broadcast_to(want[:, None], (2 * MB, 128))
        all_rows = gather_rows(spread_from_last(final_rows, section))
        return layer_out, vocab(order, all_rows, w_vocab, other_vocab, want)

    def even_path():
        return layer_rows(gather_rows(normed))[0], jnp.zeros((128, 128), F32)

    layer_out, stats = lax.cond(odd, odd_path, even_path)
    handed = over_section(layer_out, [(s, s + 1) for s in range(15)])[None]
    got = lax.all_to_all(stats, ("section", "tensor"), 0, 0, tiled=True)
    return handed, merge(got)


def solution(mesh):
    placed = (
        P("section", "tensor", None),
        P("section", None),
        P("section", None),
        P("section", None, "tensor"),
        P("section", None, "tensor", None),
        P("section", "tensor", None),
        P(),
        P(None, ("section", "tensor")),
        P(),
    )
    return jax.shard_map(
        body,
        mesh=mesh,
        in_specs=placed,
        out_specs=(P("section", "tensor", None), P("tensor")),
        check_vma=False,
    )
```

```python
import math

import jax
import jax.numpy as jnp
from jax import lax
from jax.experimental import pallas as pl
from jax.experimental.pallas import tpu as pltpu
from jax.sharding import PartitionSpec as P

NORM_EPSILON = 1e-05
ROPE_THETA = 500000.0
BF16 = jnp.bfloat16
F32 = jnp.float32
NZ = 4
ROWS = 32
HALF = 16
WIDTH = 8192
HEAD = 128
HEADS = 4
MB = 128
VL = 256


def tensor_pairs(step):
    out = []
    for x in range(2):
        for z in range(NZ):
            x2, z2 = step(x, z)
            out.append((x * NZ + z, (x2 % 2) * NZ + z2 % NZ))
    return out


TO_X = tensor_pairs(lambda x, z: (x + 1, z))
TO_UP = tensor_pairs(lambda x, z: (x, z + 1))
TO_DOWN = tensor_pairs(lambda x, z: (x, z - 1))


def sec(y, h, c):
    return ((y % 4) * 2 + h % 2) * 2 + c


def over_tensor(block, pairs):
    return lax.ppermute(block, "tensor", pairs)


def over_section(block, pairs):
    return lax.ppermute(block, "section", pairs)


def gather_first(own):
    from_x = over_tensor(own, TO_X)
    below = over_tensor(own, TO_UP)
    above = over_tensor(own, TO_DOWN)
    return above, over_tensor(below, TO_UP), below, from_x


def gather_rest(own, first):
    above, far, below, from_x = first
    x_far = over_tensor(far, TO_X)
    x_below = over_tensor(from_x, TO_UP)
    x_above = over_tensor(from_x, TO_DOWN)
    return own, above, far, below, from_x, x_above, x_far, x_below


def gather_rows(own):
    return gather_rest(own, gather_first(own))


def gather_rows_split(own):
    from_x = over_tensor(own, TO_X)
    below = over_tensor(own, TO_UP)
    above = over_tensor(own, TO_DOWN)
    far_a = over_tensor(below[:HALF], TO_UP)
    far_b = over_tensor(above[HALF:], TO_DOWN)
    x_below = over_tensor(from_x, TO_UP)
    x_above = over_tensor(from_x, TO_DOWN)
    far = jnp.concatenate([far_a, far_b])
    x_far = over_tensor(far, TO_X)
    return own, above, far, below, from_x, x_above, x_far, x_below


def gather_pairs(own):
    from_x = over_tensor(own, TO_X)
    pair = jnp.concatenate([own, from_x])
    below = over_tensor(pair, TO_UP)
    above = over_tensor(pair, TO_DOWN)
    far_a = over_tensor(below[:HALF], TO_UP)
    far_b = over_tensor(above[HALF:ROWS], TO_DOWN)
    far = jnp.concatenate([far_a, far_b])
    x_far = over_tensor(far, TO_X)
    return own, above[:ROWS], far, below[:ROWS], from_x, above[ROWS:], x_far, below[ROWS:]


def scatter_sum(parts):
    own, above, far, below, x_own, x_above, x_far, x_below = parts
    got_far = over_tensor(x_far, TO_X)
    got_x_down = over_tensor(x_above, TO_UP)
    got_x_up = over_tensor(x_below, TO_DOWN)
    far_a = add(far[:HALF], got_far[:HALF]).astype(BF16)
    far_b = add(far[HALF:], got_far[HALF:]).astype(BF16)
    got_a = over_tensor(far_a, TO_DOWN)
    got_b = over_tensor(far_b, TO_UP)
    x_own = add(x_own, got_x_down, got_x_up).astype(BF16)
    got_x = over_tensor(x_own, TO_X)
    below = jnp.concatenate([add(below[:HALF], got_a), below[HALF:].astype(F32)], axis=0).astype(BF16)
    above = jnp.concatenate([above[:HALF].astype(F32), add(above[HALF:], got_b)], axis=0).astype(BF16)
    got_down = over_tensor(below, TO_DOWN)
    got_up = over_tensor(above, TO_UP)
    return own, got_x, got_down, got_up


def norm_value(values, gain):
    factor = lax.rsqrt(jnp.mean(values * values, axis=-1, keepdims=True) + NORM_EPSILON)
    return (values * factor * gain.astype(F32)).astype(BF16)


def norm_kernel(rows_ref, gain_ref, out_ref):
    out_ref[...] = norm_value(rows_ref[...].astype(F32), gain_ref[...])


def rms_norm(rows, gain):
    return pl.pallas_call(
        norm_kernel, out_shape=jax.ShapeDtypeStruct(rows.shape, BF16), name="norm"
    )(rows, gain.reshape(1, -1))


def finish_kernel(rows_ref, a_ref, b_ref, c_ref, d_ref, gain_ref, out_ref, final_ref):
    out = add(rows_ref[...], a_ref[...], b_ref[...], c_ref[...], d_ref[...]).astype(BF16)
    out_ref[...] = out
    final_ref[...] = norm_value(out.astype(F32), gain_ref[...])


def finish(rows, terms, gain):
    return pl.pallas_call(
        finish_kernel,
        out_shape=[jax.ShapeDtypeStruct(rows.shape, BF16)] * 2,
        compiler_params=pltpu.CompilerParams(vmem_limit_bytes=24 * 1024 * 1024),
        name="finish",
    )(rows, *terms, gain.reshape(1, -1))


def merge_kernel(got_ref, out_ref):
    got = got_ref[...].reshape(8, 2, 8, 128)[:, 1].reshape(64, 128)
    tops, totals, picks = got[:, :ROWS], got[:, ROWS : 2 * ROWS], got[:, 2 * ROWS : 3 * ROWS]
    top = jnp.max(tops, axis=0, keepdims=True)
    total = jnp.sum(totals * jnp.exp(tops - top), axis=0, keepdims=True)
    out_ref[...] = (jnp.sum(picks, axis=0, keepdims=True) - top - jnp.log(total))[0]


def merge(got):
    return pl.pallas_call(
        merge_kernel, out_shape=jax.ShapeDtypeStruct((ROWS,), F32), name="merge"
    )(got)


KC = 2048
NC = 2048
QKV = (HEADS + 2) * HEAD


def at(k, size):
    return pl.ds(pl.multiple_of(k * size, size), size)


def layer_kernel(*refs):
    blocks = refs[:8]
    wq_ref, wkv_ref, wo_ref, cos_ref, sin_ref, allow_ref = refs[8:14]
    outs = refs[14:22]
    rows, w, wo, acc, ctx, row_sem, w_sem, wo_sem = refs[22:]

    for i, b in enumerate(blocks):
        pltpu.make_async_copy(b, rows.at[pl.ds(i * ROWS, ROWS)], row_sem).start()

    @pl.loop(0, WIDTH // KC)
    def _(k):
        cols = at(k, KC)
        q_cols, kv_cols = pl.ds(0, HEADS * HEAD), pl.ds(HEADS * HEAD, 2 * HEAD)
        pltpu.make_async_copy(wq_ref.at[cols], w.at[cols, q_cols], w_sem.at[k]).start()
        pltpu.make_async_copy(wkv_ref.at[cols], w.at[cols, kv_cols], w_sem.at[k]).start()

    @pl.loop(0, WIDTH // NC)
    def _(n):
        cols = at(n, NC)
        pltpu.make_async_copy(wo_ref.at[:, cols], wo.at[:, cols], wo_sem.at[n]).start()

    acc[...] = jnp.zeros_like(acc)
    pltpu.make_async_copy(rows, rows, row_sem).wait()

    @pl.loop(0, WIDTH // KC)
    def _(k):
        cols = at(k, KC)
        pltpu.make_async_copy(w.at[cols], w.at[cols], w_sem.at[k]).wait()
        acc[...] += jnp.dot(rows[:, cols], w[cols, :], preferred_element_type=F32)

    cos, sin = cos_ref[...], sin_ref[...]

    def rotated(h):
        v = acc[:, h * HEAD : (h + 1) * HEAD]
        return (v * cos + pltpu.roll(v, HEAD // 2, 1) * sin).astype(BF16)

    keys = rotated(HEADS)
    values = acc[:, (HEADS + 1) * HEAD :].astype(BF16)
    heads = [rotated(h) for h in range(HEADS)]
    for b in range(2):
        mb = slice(b * MB, (b + 1) * MB)
        allow = jnp.concatenate([allow_ref[mb, :]] * HEADS, axis=0) > 0
        q = jnp.concatenate([head[mb] for head in heads], axis=0)
        s = lax.dot_general(q, keys[mb], (((1,), (1,)), ((), ())), preferred_element_type=F32)
        s = jnp.where(allow, s * (1.0 / math.sqrt(HEAD)), -jnp.inf)
        e = jnp.exp(s - jnp.max(s, axis=1, keepdims=True))
        p = (e / jnp.sum(e, axis=1, keepdims=True)).astype(BF16)
        c = jnp.dot(p, values[mb], preferred_element_type=F32).astype(BF16)
        for h in range(HEADS):
            ctx[mb, h * HEAD : (h + 1) * HEAD] = c[h * MB : (h + 1) * MB]

    @pl.loop(0, WIDTH // NC)
    def _(n):
        cols = at(n, NC)
        pltpu.make_async_copy(wo.at[:, cols], wo.at[:, cols], wo_sem.at[n]).wait()
        part = jnp.dot(ctx[...], wo[:, cols], preferred_element_type=F32).astype(BF16)
        for i, o in enumerate(outs):
            o[:, cols] = part[i * ROWS : (i + 1) * ROWS]


def layer(blocks, wq, wkv, wo, cos, sin, allow):
    hbm = pl.BlockSpec(memory_space=pl.ANY)
    vmem = pl.BlockSpec(memory_space=pltpu.VMEM)
    return pl.pallas_call(
        layer_kernel,
        out_shape=[jax.ShapeDtypeStruct((ROWS, WIDTH), BF16)] * 8,
        in_specs=[hbm] * 11 + [vmem] * 3,
        out_specs=[vmem] * 8,
        scratch_shapes=[
            pltpu.VMEM((2 * MB, WIDTH), BF16),
            pltpu.VMEM((WIDTH, QKV), BF16),
            pltpu.VMEM((HEADS * HEAD, WIDTH), BF16),
            pltpu.VMEM((2 * MB, QKV), F32),
            pltpu.VMEM((2 * MB, HEADS * HEAD), BF16),
            pltpu.SemaphoreType.DMA,
            pltpu.SemaphoreType.DMA((WIDTH // KC,)),
            pltpu.SemaphoreType.DMA((WIDTH // NC,)),
        ],
        compiler_params=pltpu.CompilerParams(vmem_limit_bytes=48 * 1024 * 1024),
        cost_estimate=pl.CostEstimate(flops=6 * 10**9, bytes_accessed=28 * 2**20, transcendentals=0),
        name="layer",
    )(*blocks, wq, wkv, wo, cos, sin, allow)


VC = 2048


def vocab_kernel(order_ref, *refs):
    blocks = refs[:8]
    w0_ref, w1_ref, want_ref, out_ref, rows, w, acc, row_sem, w_sem = refs[8:]
    for i, b in enumerate(blocks):
        pltpu.make_async_copy(b, rows.at[pl.ds(i * ROWS, ROWS)], row_sem).start()

    @pl.loop(0, WIDTH // VC)
    def _(k):
        cols = at(k, VC)
        for i, r in enumerate((w0_ref, w1_ref)):
            pltpu.make_async_copy(r.at[cols], w.at[cols, pl.ds(i * VL, VL)], w_sem.at[k]).start()

    acc[...] = jnp.zeros_like(acc)
    pltpu.make_async_copy(rows, rows, row_sem).wait()

    @pl.loop(0, WIDTH // VC, unroll=True)
    def _(k):
        cols = at(k, VC)
        pltpu.make_async_copy(w.at[cols], w.at[cols], w_sem.at[k]).wait()
        acc[...] += jnp.dot(rows[:, cols], w[cols, :], preferred_element_type=F32)

    logits = acc[...]
    top = jnp.max(logits, axis=1, keepdims=True)
    total = jnp.sum(jnp.exp(logits - top), axis=1, keepdims=True)
    column = lax.broadcasted_iota(jnp.int32, logits.shape, 1)
    picked = jnp.sum(jnp.where(column == want_ref[:, :1], logits, 0.0), axis=1, keepdims=True)
    lane = lax.broadcasted_iota(jnp.int32, (2 * MB, 128), 1)
    stats = jnp.where(lane == 0, top, jnp.where(lane == 1, total, picked)).T
    for i in range(8):
        mine = slice(i * ROWS, (i + 1) * ROWS)
        line = jnp.concatenate([stats[k : k + 1, mine] for k in (0, 1, 2, 2)], axis=1)
        out_ref[pl.ds(order_ref[i], 1), :] = line
    lines = out_ref[:8, :]
    for s in range(1, 16):
        out_ref[s * 8 : (s + 1) * 8, :] = lines


def vocab(order, blocks, w0, w1, want):
    hbm = pl.BlockSpec(memory_space=pl.ANY)
    vmem = pl.BlockSpec(memory_space=pltpu.VMEM)
    return pl.pallas_call(
        vocab_kernel,
        out_shape=jax.ShapeDtypeStruct((128, 128), F32),
        in_specs=[pl.BlockSpec(memory_space=pltpu.SMEM)] + [hbm] * 10 + [vmem],
        out_specs=vmem,
        scratch_shapes=[
            pltpu.VMEM((2 * MB, WIDTH), BF16),
            pltpu.VMEM((WIDTH, 2 * VL), BF16),
            pltpu.VMEM((2 * MB, 2 * VL), F32),
            pltpu.SemaphoreType.DMA,
            pltpu.SemaphoreType.DMA((WIDTH // VC,)),
        ],
        compiler_params=pltpu.CompilerParams(vmem_limit_bytes=48 * 1024 * 1024),
        cost_estimate=pl.CostEstimate(flops=2 * 10**9, bytes_accessed=14 * 2**20, transcendentals=0),
        name="vocab",
    )(order, *blocks, w0, w1, want)


def add(*terms):
    return sum(t.astype(F32) for t in terms)


BESIDE = [(r, r ^ (2 * 8) ^ NZ) for r in range(128)]


def spread_from_last(final_rows, section):
    y, h = section // 4, section // 2 % 2

    def hop(to):
        return over_section(final_rows, [(15, sec(to, 1, 1))])

    up, down, across = hop(0), hop(2), hop(1)
    rows = jnp.where(y == 3, final_rows, jnp.where(y == 0, up, jnp.where(y == 2, down, across)))
    here = [(r, to) for r, to in BESIDE if r // 8 % 4 == 3]
    return jnp.where(h == 1, rows, lax.ppermute(rows, ("section", "tensor"), here))


def body(
    section_input, positions, attn_gain, w_query, w_keyval, w_out_proj, final_gain, w_vocab, targets
):
    section, rank = lax.axis_index("section"), lax.axis_index("tensor")
    core, x, z = section % 2, rank // NZ, rank % NZ
    my_rows = section_input[0]
    normed = rms_norm(my_rows, attn_gain[0])
    other_vocab = over_section(w_vocab, [(s, s ^ 1) for s in range(16)])

    zs = (z + jnp.arange(NZ)) % NZ

    def order_from(first_x):
        return (jnp.stack([first_x, 1 - first_x])[:, None] * NZ + zs[None, :]).reshape(-1)

    def tables():
        place = ((zs * ROWS)[:, None] + jnp.arange(ROWS)[None, :]).reshape(-1)
        pos = jnp.take(positions[0].reshape(8, ROWS), order_from(x), axis=0).reshape(-1)
        place2 = jnp.concatenate([place, place])
        frequency = ROPE_THETA ** (-jnp.arange(HEAD // 2, dtype=F32) * 2.0 / HEAD)
        angles = pos.astype(F32)[:, None] * frequency[None, :]
        cos, sin = jnp.cos(angles), jnp.sin(angles)
        cos = jnp.concatenate([cos, cos], axis=1)
        sin = jnp.concatenate([-sin, sin], axis=1)
        keys_at = place[None, :]
        allow = ((keys_at <= place2[:, None]) & (keys_at >= (place2 - pos)[:, None])).astype(F32)
        return cos, sin, allow

    odd = core == 1
    blank = jnp.zeros((ROWS, WIDTH), BF16)
    weights = (w_query[0], w_keyval[0].reshape(WIDTH, -1), w_out_proj[0])
    blocks, angles = lax.cond(
        odd, lambda: (gather_rows(normed)[1:], tables()), lambda: ((blank,) * 7, tables())
    )
    blocks = (normed, *blocks)

    def layer_rows(blocks):
        return finish(my_rows, scatter_sum(layer(blocks, *weights, *angles)), final_gain)

    def odd_path():
        layer_out, final_rows = layer_rows(blocks)
        order = order_from(jnp.where(section // 2 % 2 == 1, x, 1 - x))
        starts = jnp.stack([section, section ^ 1]) * 8 * VL + rank * VL
        want = jnp.take(targets.reshape(8, ROWS), order, axis=0).reshape(-1)
        local = want[:, None] - starts[None, :]
        inside = (local >= 0) & (local < VL)
        want = jnp.max(jnp.where(inside, local + jnp.arange(2)[None, :] * VL, -1), axis=1)
        want = jnp.broadcast_to(want[:, None], (2 * MB, 128))
        all_rows = gather_rows_split(spread_from_last(final_rows, section))
        return layer_out, vocab(order, all_rows, w_vocab, other_vocab, want)

    def even_path():
        return layer_rows(gather_pairs(normed))[0], jnp.zeros((128, 128), F32)

    layer_out, stats = lax.cond(odd, odd_path, even_path)
    handed = over_section(layer_out, [(s, s + 1) for s in range(15)])[None]
    got = lax.all_to_all(stats, ("section", "tensor"), 0, 0, tiled=True)
    return handed, merge(got)


def solution(mesh):
    placed = (
        P("section", "tensor", None),
        P("section", None),
        P("section", None),
        P("section", None, "tensor"),
        P("section", None, "tensor", None),
        P("section", "tensor", None),
        P(),
        P(None, ("section", "tensor")),
        P(),
    )
    return jax.shard_map(
        body,
        mesh=mesh,
        in_specs=placed,
        out_specs=(P("section", "tensor", None), P("tensor")),
        check_vma=False,
    )
```

```python
import functools
import math

import jax
import jax.numpy as jnp
from jax import lax
from jax.experimental import pallas as pl
from jax.experimental.pallas import tpu as pltpu
from jax.sharding import PartitionSpec as P

NORM_EPSILON = 1e-05
ROPE_THETA = 500000.0
BF16 = jnp.bfloat16
F32 = jnp.float32
NZ = 4
ROWS = 32
HALF = 16
WIDTH = 8192
HEAD = 128
HEADS = 4
MB = 128
VL = 256


def tensor_pairs(step):
    out = []
    for x in range(2):
        for z in range(NZ):
            x2, z2 = step(x, z)
            out.append((x * NZ + z, (x2 % 2) * NZ + z2 % NZ))
    return out


TO_X = tensor_pairs(lambda x, z: (x + 1, z))
TO_UP = tensor_pairs(lambda x, z: (x, z + 1))
TO_DOWN = tensor_pairs(lambda x, z: (x, z - 1))


def sec(y, h, c):
    return ((y % 4) * 2 + h % 2) * 2 + c


def over_tensor(block, pairs):
    return lax.ppermute(block, "tensor", pairs)


def over_section(block, pairs):
    return lax.ppermute(block, "section", pairs)


def gather_first(own):
    from_x = over_tensor(own, TO_X)
    below = over_tensor(own, TO_UP)
    above = over_tensor(own, TO_DOWN)
    return above, over_tensor(below, TO_UP), below, from_x


def gather_rest(own, first):
    above, far, below, from_x = first
    x_far = over_tensor(far, TO_X)
    x_below = over_tensor(from_x, TO_UP)
    x_above = over_tensor(from_x, TO_DOWN)
    return own, above, far, below, from_x, x_above, x_far, x_below


def gather_rows(own):
    return gather_rest(own, gather_first(own))


def gather_rows_split(own):
    from_x = over_tensor(own, TO_X)
    below = over_tensor(own, TO_UP)
    above = over_tensor(own, TO_DOWN)
    far_a = over_tensor(below[:HALF], TO_UP)
    far_b = over_tensor(above[HALF:], TO_DOWN)
    x_below = over_tensor(from_x, TO_UP)
    x_above = over_tensor(from_x, TO_DOWN)
    far = jnp.concatenate([far_a, far_b])
    x_far = over_tensor(far, TO_X)
    return own, above, far, below, from_x, x_above, x_far, x_below


def gather_pairs(own):
    from_x = over_tensor(own, TO_X)
    pair = jnp.concatenate([own, from_x])
    below = over_tensor(pair, TO_UP)
    above = over_tensor(pair, TO_DOWN)
    far_a = over_tensor(below[:HALF], TO_UP)
    far_b = over_tensor(above[HALF:ROWS], TO_DOWN)
    x_far_a = over_tensor(far_a, TO_X)
    x_far_b = over_tensor(far_b, TO_X)
    return own, above, far_a, far_b, below, from_x, x_far_a, x_far_b


def scatter_sum(parts):
    own, above, far, below, x_own, x_above, x_far, x_below = parts
    got_far = over_tensor(x_far, TO_X)
    got_x_down = over_tensor(x_above, TO_UP)
    got_x_up = over_tensor(x_below, TO_DOWN)
    far_a = add(far[:HALF], got_far[:HALF]).astype(BF16)
    far_b = add(far[HALF:], got_far[HALF:]).astype(BF16)
    got_a = over_tensor(far_a, TO_DOWN)
    got_b = over_tensor(far_b, TO_UP)
    x_own = add(x_own, got_x_down, got_x_up).astype(BF16)
    got_x = over_tensor(x_own, TO_X)
    below = jnp.concatenate([add(below[:HALF], got_a), below[HALF:].astype(F32)], axis=0).astype(BF16)
    above = jnp.concatenate([above[:HALF].astype(F32), add(above[HALF:], got_b)], axis=0).astype(BF16)
    got_down = over_tensor(below, TO_DOWN)
    got_up = over_tensor(above, TO_UP)
    return own, got_x, got_down, got_up


def norm_value(values, gain):
    factor = lax.rsqrt(jnp.mean(values * values, axis=-1, keepdims=True) + NORM_EPSILON)
    return (values * factor * gain.astype(F32)).astype(BF16)


def norm_kernel(rows_ref, gain_ref, out_ref):
    out_ref[...] = norm_value(rows_ref[...].astype(F32), gain_ref[...])


def rms_norm(rows, gain):
    return pl.pallas_call(
        norm_kernel, out_shape=jax.ShapeDtypeStruct(rows.shape, BF16), name="norm"
    )(rows, gain.reshape(1, -1))


def finish_kernel(rows_ref, a_ref, b_ref, c_ref, d_ref, gain_ref, out_ref, final_ref):
    out = add(rows_ref[...], a_ref[...], b_ref[...], c_ref[...], d_ref[...]).astype(BF16)
    out_ref[...] = out
    final_ref[...] = norm_value(out.astype(F32), gain_ref[...])


def finish(rows, terms, gain):
    return pl.pallas_call(
        finish_kernel,
        out_shape=[jax.ShapeDtypeStruct(rows.shape, BF16)] * 2,
        compiler_params=pltpu.CompilerParams(vmem_limit_bytes=24 * 1024 * 1024),
        name="finish",
    )(rows, *terms, gain.reshape(1, -1))


def merge_kernel(got_ref, out_ref):
    got = got_ref[...].reshape(8, 2, 8, 128)[:, 1].reshape(64, 128)
    tops, totals, picks = got[:, :ROWS], got[:, ROWS : 2 * ROWS], got[:, 2 * ROWS : 3 * ROWS]
    top = jnp.max(tops, axis=0, keepdims=True)
    total = jnp.sum(totals * jnp.exp(tops - top), axis=0, keepdims=True)
    out_ref[...] = (jnp.sum(picks, axis=0, keepdims=True) - top - jnp.log(total))[0]


def merge(got):
    return pl.pallas_call(
        merge_kernel, out_shape=jax.ShapeDtypeStruct((ROWS,), F32), name="merge"
    )(got)


KC = 2048
NC = 4096
QKV = (HEADS + 2) * HEAD


def at(k, size):
    return pl.ds(pl.multiple_of(k * size, size), size)


def layer_kernel(layout, *refs):
    n_blocks = 1 + max(block for block, *_ in layout)
    blocks = refs[:n_blocks]
    wq_ref, wkv_ref, wo_ref, cos_ref, sin_ref, allow_ref = refs[n_blocks : n_blocks + 6]
    outs = refs[n_blocks + 6 : n_blocks + 14]
    rows, w, wo, acc, ctx, row_sem, w_sem, wo_sem = refs[n_blocks + 14 :]

    for block, start, n, to in layout:
        pltpu.make_async_copy(
            blocks[block].at[pl.ds(start, n)], rows.at[pl.ds(to, n)], row_sem
        ).start()

    @pl.loop(0, WIDTH // KC)
    def _(k):
        cols = at(k, KC)
        q_cols, kv_cols = pl.ds(0, HEADS * HEAD), pl.ds(HEADS * HEAD, 2 * HEAD)
        pltpu.make_async_copy(wq_ref.at[cols], w.at[cols, q_cols], w_sem.at[k]).start()
        pltpu.make_async_copy(wkv_ref.at[cols], w.at[cols, kv_cols], w_sem.at[k]).start()

    @pl.loop(0, WIDTH // NC)
    def _(n):
        cols = at(n, NC)
        pltpu.make_async_copy(wo_ref.at[:, cols], wo.at[:, cols], wo_sem.at[n]).start()

    acc[...] = jnp.zeros_like(acc)
    pltpu.make_async_copy(rows, rows, row_sem).wait()

    @pl.loop(0, WIDTH // KC)
    def _(k):
        cols = at(k, KC)
        pltpu.make_async_copy(w.at[cols], w.at[cols], w_sem.at[k]).wait()
        acc[...] += jnp.dot(rows[:, cols], w[cols, :], preferred_element_type=F32)

    cos, sin = cos_ref[...], sin_ref[...]

    def rotated(h):
        v = acc[:, h * HEAD : (h + 1) * HEAD]
        return (v * cos + pltpu.roll(v, HEAD // 2, 1) * sin).astype(BF16)

    keys = rotated(HEADS)
    values = acc[:, (HEADS + 1) * HEAD :].astype(BF16)
    heads = [rotated(h) for h in range(HEADS)]
    for b in range(2):
        mb = slice(b * MB, (b + 1) * MB)
        allow = jnp.concatenate([allow_ref[mb, :]] * HEADS, axis=0) > 0
        q = jnp.concatenate([head[mb] for head in heads], axis=0)
        s = lax.dot_general(q, keys[mb], (((1,), (1,)), ((), ())), preferred_element_type=F32)
        s = jnp.where(allow, s * (1.0 / math.sqrt(HEAD)), -jnp.inf)
        e = jnp.exp(s - jnp.max(s, axis=1, keepdims=True))
        p = (e / jnp.sum(e, axis=1, keepdims=True)).astype(BF16)
        c = jnp.dot(p, values[mb], preferred_element_type=F32).astype(BF16)
        for h in range(HEADS):
            ctx[mb, h * HEAD : (h + 1) * HEAD] = c[h * MB : (h + 1) * MB]

    @pl.loop(0, WIDTH // NC)
    def _(n):
        cols = at(n, NC)
        pltpu.make_async_copy(wo.at[:, cols], wo.at[:, cols], wo_sem.at[n]).wait()
        part = jnp.dot(ctx[...], wo[:, cols], preferred_element_type=F32).astype(BF16)
        for i, o in enumerate(outs):
            o[:, cols] = part[i * ROWS : (i + 1) * ROWS]


EACH = tuple((i, 0, ROWS, i * ROWS) for i in range(8))
PAIRED = (
    (0, 0, 32, 0), (1, 0, 32, 32), (2, 0, 16, 64), (3, 0, 16, 80), (4, 0, 32, 96),
    (5, 0, 32, 128), (1, 32, 32, 160), (6, 0, 16, 192), (7, 0, 16, 208), (4, 32, 32, 224),
)


def layer(layout, blocks, wq, wkv, wo, cos, sin, allow):
    hbm = pl.BlockSpec(memory_space=pl.ANY)
    vmem = pl.BlockSpec(memory_space=pltpu.VMEM)
    return pl.pallas_call(
        functools.partial(layer_kernel, layout),
        out_shape=[jax.ShapeDtypeStruct((ROWS, WIDTH), BF16)] * 8,
        in_specs=[hbm] * (len(blocks) + 3) + [vmem] * 3,
        out_specs=[vmem] * 8,
        scratch_shapes=[
            pltpu.VMEM((2 * MB, WIDTH), BF16),
            pltpu.VMEM((WIDTH, QKV), BF16),
            pltpu.VMEM((HEADS * HEAD, WIDTH), BF16),
            pltpu.VMEM((2 * MB, QKV), F32),
            pltpu.VMEM((2 * MB, HEADS * HEAD), BF16),
            pltpu.SemaphoreType.DMA,
            pltpu.SemaphoreType.DMA((WIDTH // KC,)),
            pltpu.SemaphoreType.DMA((WIDTH // NC,)),
        ],
        compiler_params=pltpu.CompilerParams(vmem_limit_bytes=48 * 1024 * 1024),
        cost_estimate=pl.CostEstimate(flops=6 * 10**9, bytes_accessed=28 * 2**20, transcendentals=0),
        name="layer",
    )(*blocks, wq, wkv, wo, cos, sin, allow)


VC = 2048


def vocab_kernel(first, order_ref, *refs):
    blocks = refs[:NZ]
    w0_ref, w1_ref, want_ref = refs[NZ : NZ + 3]
    out_ref, rows, w, acc, row_sem, w_sem = refs[-6:]
    for i, b in enumerate(blocks):
        pltpu.make_async_copy(b, rows.at[pl.ds(i * ROWS, ROWS)], row_sem).start()

    @pl.loop(0, WIDTH // VC)
    def _(k):
        cols = at(k, VC)
        for i, r in enumerate((w0_ref, w1_ref)):
            pltpu.make_async_copy(r.at[cols], w.at[cols, pl.ds(i * VL, VL)], w_sem.at[k]).start()

    acc[...] = jnp.zeros_like(acc)
    pltpu.make_async_copy(rows, rows, row_sem).wait()

    @pl.loop(0, WIDTH // VC, unroll=True)
    def _(k):
        cols = at(k, VC)
        pltpu.make_async_copy(w.at[cols], w.at[cols], w_sem.at[k]).wait()
        acc[...] += jnp.dot(rows[:, cols], w[cols, :], preferred_element_type=F32)

    logits = acc[...]
    top = jnp.max(logits, axis=1, keepdims=True)
    total = jnp.sum(jnp.exp(logits - top), axis=1, keepdims=True)
    column = lax.broadcasted_iota(jnp.int32, logits.shape, 1)
    want = want_ref[first * ROWS : (first + NZ) * ROWS, :1]
    picked = jnp.sum(jnp.where(column == want, logits, 0.0), axis=1, keepdims=True)
    lane = lax.broadcasted_iota(jnp.int32, (MB, 128), 1)
    stats = jnp.where(lane == 0, top, jnp.where(lane == 1, total, picked)).T
    if first:
        out_ref[:8, :] = refs[NZ + 3][...]
    for i in range(NZ):
        mine = slice(i * ROWS, (i + 1) * ROWS)
        line = jnp.concatenate([stats[k : k + 1, mine] for k in (0, 1, 2, 2)], axis=1)
        out_ref[pl.ds(order_ref[first + i], 1), :] = line
    if first:
        lines = out_ref[:8, :]
        for s in range(1, 16):
            out_ref[s * 8 : (s + 1) * 8, :] = lines


def vocab_part(order, blocks, w0, w1, want, lines=None):
    hbm = pl.BlockSpec(memory_space=pl.ANY)
    vmem = pl.BlockSpec(memory_space=pltpu.VMEM)
    given = [] if lines is None else [lines]
    return pl.pallas_call(
        functools.partial(vocab_kernel, NZ * len(given)),
        out_shape=jax.ShapeDtypeStruct((128 if given else 8, 128), F32),
        in_specs=[pl.BlockSpec(memory_space=pltpu.SMEM)] + [hbm] * (NZ + 2) + [vmem] * (1 + len(given)),
        out_specs=vmem,
        scratch_shapes=[
            pltpu.VMEM((MB, WIDTH), BF16),
            pltpu.VMEM((WIDTH, 2 * VL), BF16),
            pltpu.VMEM((MB, 2 * VL), F32),
            pltpu.SemaphoreType.DMA,
            pltpu.SemaphoreType.DMA((WIDTH // VC,)),
        ],
        compiler_params=pltpu.CompilerParams(vmem_limit_bytes=32 * 1024 * 1024),
        cost_estimate=pl.CostEstimate(flops=10**9, bytes_accessed=10 * 2**20, transcendentals=0),
        name="vocab",
    )(order, *blocks, w0, w1, want, *given)


def vocab(order, blocks, w0, w1, want):
    lines = vocab_part(order, blocks[:NZ], w0, w1, want)
    return vocab_part(order, blocks[NZ:], w0, w1, want, lines)


def add(*terms):
    return sum(t.astype(F32) for t in terms)


BESIDE = [(r, r ^ (2 * 8) ^ NZ) for r in range(128)]


def spread_from_last(final_rows, section):
    y, h = section // 4, section // 2 % 2

    def hop(to):
        return over_section(final_rows, [(15, sec(to, 1, 1))])

    up, down, across = hop(0), hop(2), hop(1)
    rows = jnp.where(y == 3, final_rows, jnp.where(y == 0, up, jnp.where(y == 2, down, across)))
    here = [(r, to) for r, to in BESIDE if r // 8 % 4 == 3]
    return jnp.where(h == 1, rows, lax.ppermute(rows, ("section", "tensor"), here))


def body(
    section_input, positions, attn_gain, w_query, w_keyval, w_out_proj, final_gain, w_vocab, targets
):
    section, rank = lax.axis_index("section"), lax.axis_index("tensor")
    core, x, z = section % 2, rank // NZ, rank % NZ
    my_rows = section_input[0]
    normed = rms_norm(my_rows, attn_gain[0])
    other_vocab = over_section(w_vocab, [(s, s ^ 1) for s in range(16)])

    zs = (z + jnp.arange(NZ)) % NZ

    def order_from(first_x):
        return (jnp.stack([first_x, 1 - first_x])[:, None] * NZ + zs[None, :]).reshape(-1)

    def tables():
        place = ((zs * ROWS)[:, None] + jnp.arange(ROWS)[None, :]).reshape(-1)
        pos = jnp.take(positions[0].reshape(8, ROWS), order_from(x), axis=0).reshape(-1)
        place2 = jnp.concatenate([place, place])
        frequency = ROPE_THETA ** (-jnp.arange(HEAD // 2, dtype=F32) * 2.0 / HEAD)
        angles = pos.astype(F32)[:, None] * frequency[None, :]
        cos, sin = jnp.cos(angles), jnp.sin(angles)
        cos = jnp.concatenate([cos, cos], axis=1)
        sin = jnp.concatenate([-sin, sin], axis=1)
        keys_at = place[None, :]
        allow = ((keys_at <= place2[:, None]) & (keys_at >= (place2 - pos)[:, None])).astype(F32)
        return cos, sin, allow

    odd = core == 1
    blank = jnp.zeros((ROWS, WIDTH), BF16)
    weights = (w_query[0], w_keyval[0].reshape(WIDTH, -1), w_out_proj[0])
    blocks, angles = lax.cond(
        odd, lambda: (gather_rows(normed)[1:], tables()), lambda: ((blank,) * 7, tables())
    )
    blocks = (normed, *blocks)

    def layer_rows(layout, blocks):
        terms = scatter_sum(layer(layout, blocks, *weights, *angles))
        return finish(my_rows, terms, final_gain)

    def odd_path():
        layer_out, final_rows = layer_rows(EACH, blocks)
        order = order_from(jnp.where(section // 2 % 2 == 1, x, 1 - x))
        starts = jnp.stack([section, section ^ 1]) * 8 * VL + rank * VL
        want = jnp.take(targets.reshape(8, ROWS), order, axis=0).reshape(-1)
        local = want[:, None] - starts[None, :]
        inside = (local >= 0) & (local < VL)
        want = jnp.max(jnp.where(inside, local + jnp.arange(2)[None, :] * VL, -1), axis=1)
        want = jnp.broadcast_to(want[:, None], (2 * MB, 128))
        all_rows = gather_rows_split(spread_from_last(final_rows, section))
        return layer_out, vocab(order, all_rows, w_vocab, other_vocab, want)

    def even_path():
        return layer_rows(PAIRED, gather_pairs(normed))[0], jnp.zeros((128, 128), F32)

    layer_out, stats = lax.cond(odd, odd_path, even_path)
    handed = over_section(layer_out[None], [(s, s + 1) for s in range(15)])
    got = lax.all_to_all(stats, ("section", "tensor"), 0, 0, tiled=True)
    return handed, merge(got)


def solution(mesh):
    placed = (
        P("section", "tensor", None),
        P("section", None),
        P("section", None),
        P("section", None, "tensor"),
        P("section", None, "tensor", None),
        P("section", "tensor", None),
        P(),
        P(None, ("section", "tensor")),
        P(),
    )
    return jax.shard_map(
        body,
        mesh=mesh,
        in_specs=placed,
        out_specs=(P("section", "tensor", None), P("tensor")),
        check_vma=False,
    )
```

```python
import functools
import math

import jax
import jax.numpy as jnp
from jax import lax
from jax.experimental import pallas as pl
from jax.experimental.pallas import tpu as pltpu
from jax.sharding import PartitionSpec as P

NORM_EPSILON = 1e-05
ROPE_THETA = 500000.0
BF16 = jnp.bfloat16
F32 = jnp.float32
NZ = 4
ROWS = 32
HALF = 16
WIDTH = 8192
HEAD = 128
HEADS = 4
MB = 128
VL = 256


def tensor_pairs(step):
    out = []
    for x in range(2):
        for z in range(NZ):
            x2, z2 = step(x, z)
            out.append((x * NZ + z, (x2 % 2) * NZ + z2 % NZ))
    return out


TO_X = tensor_pairs(lambda x, z: (x + 1, z))
TO_UP = tensor_pairs(lambda x, z: (x, z + 1))
TO_DOWN = tensor_pairs(lambda x, z: (x, z - 1))


def sec(y, h, c):
    return ((y % 4) * 2 + h % 2) * 2 + c


def over_tensor(block, pairs):
    return lax.ppermute(block, "tensor", pairs)


def over_section(block, pairs):
    return lax.ppermute(block, "section", pairs)


def gather_first(own):
    from_x = over_tensor(own, TO_X)
    below = over_tensor(own, TO_UP)
    above = over_tensor(own, TO_DOWN)
    return above, over_tensor(below, TO_UP), below, from_x


def gather_rest(own, first):
    above, far, below, from_x = first
    x_far = over_tensor(far, TO_X)
    x_below = over_tensor(from_x, TO_UP)
    x_above = over_tensor(from_x, TO_DOWN)
    return own, above, far, below, from_x, x_above, x_far, x_below


def gather_rows(own):
    return gather_rest(own, gather_first(own))


def gather_pairs(own):
    from_x = over_tensor(own, TO_X)
    pair = jnp.concatenate([own, from_x])
    below = over_tensor(pair, TO_UP)
    above = over_tensor(pair, TO_DOWN)
    far_a = over_tensor(below[:HALF], TO_UP)
    far_b = over_tensor(above[HALF:ROWS], TO_DOWN)
    x_far_a = over_tensor(far_a, TO_X)
    x_far_b = over_tensor(far_b, TO_X)
    return own, above, far_a, far_b, below, from_x, x_far_a, x_far_b


def scatter_sum(parts):
    own, above, far, below, x_own, x_above, x_far, x_below = parts
    got_far = over_tensor(x_far, TO_X)
    got_x_down = over_tensor(x_above, TO_UP)
    got_x_up = over_tensor(x_below, TO_DOWN)
    far_a = add(far[:HALF], got_far[:HALF]).astype(BF16)
    far_b = add(far[HALF:], got_far[HALF:]).astype(BF16)
    got_a = over_tensor(far_a, TO_DOWN)
    got_b = over_tensor(far_b, TO_UP)
    x_own = add(x_own, got_x_down, got_x_up).astype(BF16)
    got_x = over_tensor(x_own, TO_X)
    below = jnp.concatenate([add(below[:HALF], got_a), below[HALF:].astype(F32)], axis=0).astype(BF16)
    above = jnp.concatenate([above[:HALF].astype(F32), add(above[HALF:], got_b)], axis=0).astype(BF16)
    got_down = over_tensor(below, TO_DOWN)
    got_up = over_tensor(above, TO_UP)
    return own, got_x, got_down, got_up


def norm_value(values, gain):
    factor = lax.rsqrt(jnp.mean(values * values, axis=-1, keepdims=True) + NORM_EPSILON)
    return (values * factor * gain.astype(F32)).astype(BF16)


def norm_kernel(rows_ref, gain_ref, out_ref):
    out_ref[...] = norm_value(rows_ref[...].astype(F32), gain_ref[...])


def rms_norm(rows, gain):
    return pl.pallas_call(
        norm_kernel, out_shape=jax.ShapeDtypeStruct(rows.shape, BF16), name="norm"
    )(rows, gain.reshape(1, -1))


def finish_kernel(rows_ref, a_ref, b_ref, c_ref, d_ref, gain_ref, out_ref, final_ref):
    out = add(rows_ref[...], a_ref[...], b_ref[...], c_ref[...], d_ref[...]).astype(BF16)
    out_ref[...] = out
    final_ref[...] = norm_value(out.astype(F32), gain_ref[...])


def finish(rows, terms, gain):
    return pl.pallas_call(
        finish_kernel,
        out_shape=[jax.ShapeDtypeStruct(rows.shape, BF16)] * 2,
        compiler_params=pltpu.CompilerParams(vmem_limit_bytes=24 * 1024 * 1024),
        name="finish",
    )(rows, *terms, gain.reshape(1, -1))


def merge_kernel(got_ref, out_ref):
    got = got_ref[...].reshape(8, 2, 8, 128)[:, 1].reshape(64, 128)
    tops, totals, picks = got[:, :ROWS], got[:, ROWS : 2 * ROWS], got[:, 2 * ROWS : 3 * ROWS]
    top = jnp.max(tops, axis=0, keepdims=True)
    total = jnp.sum(totals * jnp.exp(tops - top), axis=0, keepdims=True)
    out_ref[...] = (jnp.sum(picks, axis=0, keepdims=True) - top - jnp.log(total))[0]


def merge(got):
    return pl.pallas_call(
        merge_kernel, out_shape=jax.ShapeDtypeStruct((ROWS,), F32), name="merge"
    )(got)


KC = 2048
NC = 4096
QKV = (HEADS + 2) * HEAD


def at(k, size):
    return pl.ds(pl.multiple_of(k * size, size), size)


def layer_kernel(layout, *refs):
    n_blocks = 1 + max(block for block, *_ in layout)
    blocks = refs[:n_blocks]
    wq_ref, wkv_ref, wo_ref, cos_ref, sin_ref, allow_ref = refs[n_blocks : n_blocks + 6]
    outs = refs[n_blocks + 6 : n_blocks + 14]
    rows, w, wo, acc, ctx, row_sem, w_sem, wo_sem = refs[n_blocks + 14 :]

    for block, start, n, to in layout:
        pltpu.make_async_copy(
            blocks[block].at[pl.ds(start, n)], rows.at[pl.ds(to, n)], row_sem
        ).start()

    @pl.loop(0, WIDTH // KC)
    def _(k):
        cols = at(k, KC)
        q_cols, kv_cols = pl.ds(0, HEADS * HEAD), pl.ds(HEADS * HEAD, 2 * HEAD)
        pltpu.make_async_copy(wq_ref.at[cols], w.at[cols, q_cols], w_sem.at[k]).start()
        pltpu.make_async_copy(wkv_ref.at[cols], w.at[cols, kv_cols], w_sem.at[k]).start()

    @pl.loop(0, WIDTH // NC)
    def _(n):
        cols = at(n, NC)
        pltpu.make_async_copy(wo_ref.at[:, cols], wo.at[:, cols], wo_sem.at[n]).start()

    acc[...] = jnp.zeros_like(acc)
    pltpu.make_async_copy(rows, rows, row_sem).wait()

    @pl.loop(0, WIDTH // KC)
    def _(k):
        cols = at(k, KC)
        pltpu.make_async_copy(w.at[cols], w.at[cols], w_sem.at[k]).wait()
        acc[...] += jnp.dot(rows[:, cols], w[cols, :], preferred_element_type=F32)

    cos, sin = cos_ref[...], sin_ref[...]

    def rotated(h):
        v = acc[:, h * HEAD : (h + 1) * HEAD]
        return (v * cos + pltpu.roll(v, HEAD // 2, 1) * sin).astype(BF16)

    keys = rotated(HEADS)
    values = acc[:, (HEADS + 1) * HEAD :].astype(BF16)
    heads = [rotated(h) for h in range(HEADS)]
    for b in range(2):
        mb = slice(b * MB, (b + 1) * MB)
        allow = jnp.concatenate([allow_ref[mb, :]] * HEADS, axis=0) > 0
        q = jnp.concatenate([head[mb] for head in heads], axis=0)
        s = lax.dot_general(q, keys[mb], (((1,), (1,)), ((), ())), preferred_element_type=F32)
        s = jnp.where(allow, s * (1.0 / math.sqrt(HEAD)), -jnp.inf)
        e = jnp.exp(s - jnp.max(s, axis=1, keepdims=True))
        p = (e / jnp.sum(e, axis=1, keepdims=True)).astype(BF16)
        c = jnp.dot(p, values[mb], preferred_element_type=F32).astype(BF16)
        for h in range(HEADS):
            ctx[mb, h * HEAD : (h + 1) * HEAD] = c[h * MB : (h + 1) * MB]

    @pl.loop(0, WIDTH // NC)
    def _(n):
        cols = at(n, NC)
        pltpu.make_async_copy(wo.at[:, cols], wo.at[:, cols], wo_sem.at[n]).wait()
        part = jnp.dot(ctx[...], wo[:, cols], preferred_element_type=F32).astype(BF16)
        for i, o in enumerate(outs):
            o[:, cols] = part[i * ROWS : (i + 1) * ROWS]


EACH = tuple((i, 0, ROWS, i * ROWS) for i in range(8))
PAIRED = (
    (0, 0, 32, 0), (1, 0, 32, 32), (2, 0, 16, 64), (3, 0, 16, 80), (4, 0, 32, 96),
    (5, 0, 32, 128), (1, 32, 32, 160), (6, 0, 16, 192), (7, 0, 16, 208), (4, 32, 32, 224),
)


def layer(layout, blocks, wq, wkv, wo, cos, sin, allow):
    hbm = pl.BlockSpec(memory_space=pl.ANY)
    vmem = pl.BlockSpec(memory_space=pltpu.VMEM)
    return pl.pallas_call(
        functools.partial(layer_kernel, layout),
        out_shape=[jax.ShapeDtypeStruct((ROWS, WIDTH), BF16)] * 8,
        in_specs=[hbm] * (len(blocks) + 3) + [vmem] * 3,
        out_specs=[vmem] * 8,
        scratch_shapes=[
            pltpu.VMEM((2 * MB, WIDTH), BF16),
            pltpu.VMEM((WIDTH, QKV), BF16),
            pltpu.VMEM((HEADS * HEAD, WIDTH), BF16),
            pltpu.VMEM((2 * MB, QKV), F32),
            pltpu.VMEM((2 * MB, HEADS * HEAD), BF16),
            pltpu.SemaphoreType.DMA,
            pltpu.SemaphoreType.DMA((WIDTH // KC,)),
            pltpu.SemaphoreType.DMA((WIDTH // NC,)),
        ],
        compiler_params=pltpu.CompilerParams(vmem_limit_bytes=48 * 1024 * 1024),
        cost_estimate=pl.CostEstimate(flops=6 * 10**9, bytes_accessed=28 * 2**20, transcendentals=0),
        name="layer",
    )(*blocks, wq, wkv, wo, cos, sin, allow)


VC = 2048


def vocab_kernel(first, order_ref, *refs):
    blocks = refs[:NZ]
    w0_ref, w1_ref, want_ref = refs[NZ : NZ + 3]
    out_ref, rows, w, acc, row_sem, w_sem = refs[-6:]
    for i, b in enumerate(blocks):
        pltpu.make_async_copy(b, rows.at[pl.ds(i * ROWS, ROWS)], row_sem).start()

    @pl.loop(0, WIDTH // VC)
    def _(k):
        cols = at(k, VC)
        for i, r in enumerate((w0_ref, w1_ref)):
            pltpu.make_async_copy(r.at[cols], w.at[cols, pl.ds(i * VL, VL)], w_sem.at[k]).start()

    acc[...] = jnp.zeros_like(acc)
    pltpu.make_async_copy(rows, rows, row_sem).wait()

    @pl.loop(0, WIDTH // VC, unroll=True)
    def _(k):
        cols = at(k, VC)
        pltpu.make_async_copy(w.at[cols], w.at[cols], w_sem.at[k]).wait()
        acc[...] += jnp.dot(rows[:, cols], w[cols, :], preferred_element_type=F32)

    logits = acc[...]
    top = jnp.max(logits, axis=1, keepdims=True)
    total = jnp.sum(jnp.exp(logits - top), axis=1, keepdims=True)
    column = lax.broadcasted_iota(jnp.int32, logits.shape, 1)
    want = want_ref[first * ROWS : (first + NZ) * ROWS, :1]
    picked = jnp.sum(jnp.where(column == want, logits, 0.0), axis=1, keepdims=True)
    lane = lax.broadcasted_iota(jnp.int32, (MB, 128), 1)
    stats = jnp.where(lane == 0, top, jnp.where(lane == 1, total, picked)).T
    if first:
        out_ref[:8, :] = refs[NZ + 3][...]
    for i in range(NZ):
        mine = slice(i * ROWS, (i + 1) * ROWS)
        line = jnp.concatenate([stats[k : k + 1, mine] for k in (0, 1, 2, 2)], axis=1)
        out_ref[pl.ds(order_ref[first + i], 1), :] = line
    if first:
        lines = out_ref[:8, :]
        for s in range(1, 16):
            out_ref[s * 8 : (s + 1) * 8, :] = lines


def vocab_part(order, blocks, w0, w1, want, lines=None):
    hbm = pl.BlockSpec(memory_space=pl.ANY)
    vmem = pl.BlockSpec(memory_space=pltpu.VMEM)
    given = [] if lines is None else [lines]
    return pl.pallas_call(
        functools.partial(vocab_kernel, NZ * len(given)),
        out_shape=jax.ShapeDtypeStruct((128 if given else 8, 128), F32),
        in_specs=[pl.BlockSpec(memory_space=pltpu.SMEM)] + [hbm] * (NZ + 2) + [vmem] * (1 + len(given)),
        out_specs=vmem,
        scratch_shapes=[
            pltpu.VMEM((MB, WIDTH), BF16),
            pltpu.VMEM((WIDTH, 2 * VL), BF16),
            pltpu.VMEM((MB, 2 * VL), F32),
            pltpu.SemaphoreType.DMA,
            pltpu.SemaphoreType.DMA((WIDTH // VC,)),
        ],
        compiler_params=pltpu.CompilerParams(vmem_limit_bytes=32 * 1024 * 1024),
        cost_estimate=pl.CostEstimate(flops=10**9, bytes_accessed=10 * 2**20, transcendentals=0),
        name="vocab",
    )(order, *blocks, w0, w1, want, *given)


def vocab(order, blocks, w0, w1, want):
    lines = vocab_part(order, blocks[:NZ], w0, w1, want)
    return vocab_part(order, blocks[NZ:], w0, w1, want, lines)


def add(*terms):
    return sum(t.astype(F32) for t in terms)


BESIDE = [(r, r ^ (2 * 8) ^ NZ) for r in range(128)]


def spread_from_last(final_rows, section):
    y, h = section // 4, section // 2 % 2

    def hop(to):
        return over_section(final_rows, [(15, sec(to, 1, 1))])

    up, down, across = hop(0), hop(2), hop(1)
    rows = jnp.where(y == 3, final_rows, jnp.where(y == 0, up, jnp.where(y == 2, down, across)))
    here = [(r, to) for r, to in BESIDE if r // 8 % 4 == 3]
    return jnp.where(h == 1, rows, lax.ppermute(rows, ("section", "tensor"), here))


def body(
    section_input, positions, attn_gain, w_query, w_keyval, w_out_proj, final_gain, w_vocab, targets
):
    section, rank = lax.axis_index("section"), lax.axis_index("tensor")
    core, x, z = section % 2, rank // NZ, rank % NZ
    my_rows = section_input[0]
    normed = rms_norm(my_rows, attn_gain[0])
    other_vocab = over_section(w_vocab, [(s, s ^ 1) for s in range(16)])

    zs = (z + jnp.arange(NZ)) % NZ

    def order_from(first_x):
        return (jnp.stack([first_x, 1 - first_x])[:, None] * NZ + zs[None, :]).reshape(-1)

    def tables():
        place = ((zs * ROWS)[:, None] + jnp.arange(ROWS)[None, :]).reshape(-1)
        pos = jnp.take(positions[0].reshape(8, ROWS), order_from(x), axis=0).reshape(-1)
        place2 = jnp.concatenate([place, place])
        frequency = ROPE_THETA ** (-jnp.arange(HEAD // 2, dtype=F32) * 2.0 / HEAD)
        angles = pos.astype(F32)[:, None] * frequency[None, :]
        cos, sin = jnp.cos(angles), jnp.sin(angles)
        cos = jnp.concatenate([cos, cos], axis=1)
        sin = jnp.concatenate([-sin, sin], axis=1)
        keys_at = place[None, :]
        allow = ((keys_at <= place2[:, None]) & (keys_at >= (place2 - pos)[:, None])).astype(F32)
        return cos, sin, allow

    odd = core == 1
    blank = jnp.zeros((ROWS, WIDTH), BF16)
    weights = (w_query[0], w_keyval[0].reshape(WIDTH, -1), w_out_proj[0])
    blocks, angles = lax.cond(
        odd, lambda: (gather_rows(normed)[1:], tables()), lambda: ((blank,) * 7, tables())
    )
    blocks = (normed, *blocks)

    def layer_rows(layout, blocks):
        terms = scatter_sum(layer(layout, blocks, *weights, *angles))
        return finish(my_rows, terms, final_gain)

    def odd_path():
        layer_out, final_rows = layer_rows(EACH, blocks)
        order = order_from(jnp.where(section // 2 % 2 == 1, x, 1 - x))
        starts = jnp.stack([section, section ^ 1]) * 8 * VL + rank * VL
        want = jnp.take(targets.reshape(8, ROWS), order, axis=0).reshape(-1)
        local = want[:, None] - starts[None, :]
        inside = (local >= 0) & (local < VL)
        want = jnp.max(jnp.where(inside, local + jnp.arange(2)[None, :] * VL, -1), axis=1)
        want = jnp.broadcast_to(want[:, None], (2 * MB, 128))
        all_rows = gather_rows(spread_from_last(final_rows, section))
        return layer_out, vocab(order, all_rows, w_vocab, other_vocab, want)

    def even_path():
        return layer_rows(PAIRED, gather_pairs(normed))[0], jnp.zeros((128, 128), F32)

    layer_out, stats = lax.cond(odd, odd_path, even_path)
    handed = over_section(layer_out[None], [(s, s + 1) for s in range(15)])
    got = lax.all_to_all(stats, ("section", "tensor"), 0, 0, tiled=True)
    return handed, merge(got)


def solution(mesh):
    placed = (
        P("section", "tensor", None),
        P("section", None),
        P("section", None),
        P("section", None, "tensor"),
        P("section", None, "tensor", None),
        P("section", "tensor", None),
        P(),
        P(None, ("section", "tensor")),
        P(),
    )
    return jax.shard_map(
        body,
        mesh=mesh,
        in_specs=placed,
        out_specs=(P("section", "tensor", None), P("tensor")),
        check_vma=False,
    )
```

```python
import functools
import math

import jax
import jax.numpy as jnp
from jax import lax
from jax.experimental import pallas as pl
from jax.experimental.pallas import tpu as pltpu
from jax.sharding import PartitionSpec as P

NORM_EPSILON = 1e-05
ROPE_THETA = 500000.0
BF16 = jnp.bfloat16
F32 = jnp.float32
NZ = 4
ROWS = 32
HALF = 16
WIDTH = 8192
HEAD = 128
HEADS = 4
MB = 128
VL = 256


def tensor_pairs(step):
    out = []
    for x in range(2):
        for z in range(NZ):
            x2, z2 = step(x, z)
            out.append((x * NZ + z, (x2 % 2) * NZ + z2 % NZ))
    return out


TO_X = tensor_pairs(lambda x, z: (x + 1, z))
TO_UP = tensor_pairs(lambda x, z: (x, z + 1))
TO_DOWN = tensor_pairs(lambda x, z: (x, z - 1))


def sec(y, h, c):
    return ((y % 4) * 2 + h % 2) * 2 + c


def over_tensor(block, pairs):
    return lax.ppermute(block, "tensor", pairs)


def over_section(block, pairs):
    return lax.ppermute(block, "section", pairs)


def gather_first(own):
    from_x = over_tensor(own, TO_X)
    below = over_tensor(own, TO_UP)
    above = over_tensor(own, TO_DOWN)
    return above, over_tensor(below, TO_UP), below, from_x


def gather_rest(own, first):
    above, far, below, from_x = first
    x_far = over_tensor(far, TO_X)
    x_below = over_tensor(from_x, TO_UP)
    x_above = over_tensor(from_x, TO_DOWN)
    return own, above, far, below, from_x, x_above, x_far, x_below


def gather_rows(own):
    return gather_rest(own, gather_first(own))


def gather_pairs(own):
    from_x = over_tensor(own, TO_X)
    pair = jnp.concatenate([own, from_x])
    below = over_tensor(pair, TO_UP)
    above = over_tensor(pair, TO_DOWN)
    far_a = over_tensor(below[:HALF], TO_UP)
    far_b = over_tensor(above[HALF:ROWS], TO_DOWN)
    x_far_a = over_tensor(far_a, TO_X)
    x_far_b = over_tensor(far_b, TO_X)
    return own, above, far_a, far_b, below, from_x, x_far_a, x_far_b


def scatter_sum(parts):
    own, above, far, below, x_own, x_above, x_far, x_below = parts
    got_far = over_tensor(x_far, TO_X)
    got_x_down = over_tensor(x_above, TO_UP)
    got_x_up = over_tensor(x_below, TO_DOWN)
    far_a = add(far[:HALF], got_far[:HALF]).astype(BF16)
    far_b = add(far[HALF:], got_far[HALF:]).astype(BF16)
    got_a = over_tensor(far_a, TO_DOWN)
    got_b = over_tensor(far_b, TO_UP)
    x_own = add(x_own, got_x_down, got_x_up).astype(BF16)
    got_x = over_tensor(x_own, TO_X)
    below = jnp.concatenate([add(below[:HALF], got_a), below[HALF:].astype(F32)], axis=0).astype(BF16)
    above = jnp.concatenate([above[:HALF].astype(F32), add(above[HALF:], got_b)], axis=0).astype(BF16)
    got_down = over_tensor(below, TO_DOWN)
    got_up = over_tensor(above, TO_UP)
    return own, got_x, got_down, got_up


def norm_value(values, gain):
    factor = lax.rsqrt(jnp.mean(values * values, axis=-1, keepdims=True) + NORM_EPSILON)
    return (values * factor * gain.astype(F32)).astype(BF16)


def norm_kernel(rows_ref, gain_ref, out_ref):
    out_ref[...] = norm_value(rows_ref[...].astype(F32), gain_ref[...])


def rms_norm(rows, gain):
    return pl.pallas_call(
        norm_kernel, out_shape=jax.ShapeDtypeStruct(rows.shape, BF16), name="norm"
    )(rows, gain.reshape(1, -1))


def finish_kernel(rows_ref, a_ref, b_ref, c_ref, d_ref, gain_ref, out_ref, final_ref):
    out = add(rows_ref[...], a_ref[...], b_ref[...], c_ref[...], d_ref[...]).astype(BF16)
    out_ref[...] = out
    final_ref[...] = norm_value(out.astype(F32), gain_ref[...])


def finish(rows, terms, gain):
    return pl.pallas_call(
        finish_kernel,
        out_shape=[jax.ShapeDtypeStruct(rows.shape, BF16)] * 2,
        compiler_params=pltpu.CompilerParams(vmem_limit_bytes=24 * 1024 * 1024),
        name="finish",
    )(rows, *terms, gain.reshape(1, -1))


def merge_kernel(got_ref, out_ref):
    got = got_ref[...].reshape(8, 2, 8, 128)[:, 1].reshape(64, 128)
    tops, totals, picks = got[:, :ROWS], got[:, ROWS : 2 * ROWS], got[:, 2 * ROWS : 3 * ROWS]
    top = jnp.max(tops, axis=0, keepdims=True)
    total = jnp.sum(totals * jnp.exp(tops - top), axis=0, keepdims=True)
    out_ref[...] = (jnp.sum(picks, axis=0, keepdims=True) - top - jnp.log(total))[0]


def merge(got):
    return pl.pallas_call(
        merge_kernel, out_shape=jax.ShapeDtypeStruct((ROWS,), F32), name="merge"
    )(got)


KC = 2048
NC = 4096
QKV = (HEADS + 2) * HEAD


def at(k, size):
    return pl.ds(pl.multiple_of(k * size, size), size)


def layer_kernel(layout, *refs):
    n_blocks = 1 + max(block for block, *_ in layout)
    blocks = refs[:n_blocks]
    wq_ref, wkv_ref, wo_ref, cos_ref, sin_ref, allow_ref = refs[n_blocks : n_blocks + 6]
    outs = refs[n_blocks + 6 : n_blocks + 14]
    rows, w, wo, acc, ctx, row_sem, w_sem, wo_sem = refs[n_blocks + 14 :]

    for block, start, n, to in layout:
        pltpu.make_async_copy(
            blocks[block].at[pl.ds(start, n)], rows.at[pl.ds(to, n)], row_sem
        ).start()

    @pl.loop(0, WIDTH // KC)
    def _(k):
        cols = at(k, KC)
        q_cols, kv_cols = pl.ds(0, HEADS * HEAD), pl.ds(HEADS * HEAD, 2 * HEAD)
        pltpu.make_async_copy(wq_ref.at[cols], w.at[cols, q_cols], w_sem.at[k]).start()
        pltpu.make_async_copy(wkv_ref.at[cols], w.at[cols, kv_cols], w_sem.at[k]).start()

    @pl.loop(0, WIDTH // NC)
    def _(n):
        cols = at(n, NC)
        pltpu.make_async_copy(wo_ref.at[:, cols], wo.at[:, cols], wo_sem.at[n]).start()

    acc[...] = jnp.zeros_like(acc)
    pltpu.make_async_copy(rows, rows, row_sem).wait()

    @pl.loop(0, WIDTH // KC)
    def _(k):
        cols = at(k, KC)
        pltpu.make_async_copy(w.at[cols], w.at[cols], w_sem.at[k]).wait()
        acc[...] += jnp.dot(rows[:, cols], w[cols, :], preferred_element_type=F32)

    cos, sin = cos_ref[...], sin_ref[...]

    def rotated(h):
        v = acc[:, h * HEAD : (h + 1) * HEAD]
        return (v * cos + pltpu.roll(v, HEAD // 2, 1) * sin).astype(BF16)

    keys = rotated(HEADS)
    values = acc[:, (HEADS + 1) * HEAD :].astype(BF16)
    heads = [rotated(h) for h in range(HEADS)]
    for b in range(2):
        mb = slice(b * MB, (b + 1) * MB)
        allow = jnp.concatenate([allow_ref[mb, :]] * HEADS, axis=0) > 0
        q = jnp.concatenate([head[mb] for head in heads], axis=0)
        s = lax.dot_general(q, keys[mb], (((1,), (1,)), ((), ())), preferred_element_type=F32)
        s = jnp.where(allow, s * (1.0 / math.sqrt(HEAD)), -jnp.inf)
        e = jnp.exp(s - jnp.max(s, axis=1, keepdims=True))
        p = (e / jnp.sum(e, axis=1, keepdims=True)).astype(BF16)
        c = jnp.dot(p, values[mb], preferred_element_type=F32).astype(BF16)
        for h in range(HEADS):
            ctx[mb, h * HEAD : (h + 1) * HEAD] = c[h * MB : (h + 1) * MB]

    @pl.loop(0, WIDTH // NC)
    def _(n):
        cols = at(n, NC)
        pltpu.make_async_copy(wo.at[:, cols], wo.at[:, cols], wo_sem.at[n]).wait()
        part = jnp.dot(ctx[...], wo[:, cols], preferred_element_type=F32).astype(BF16)
        for i, o in enumerate(outs):
            o[:, cols] = part[i * ROWS : (i + 1) * ROWS]


EACH = tuple((i, 0, ROWS, i * ROWS) for i in range(8))
PAIRED = (
    (0, 0, 32, 0), (1, 0, 32, 32), (2, 0, 16, 64), (3, 0, 16, 80), (4, 0, 32, 96),
    (5, 0, 32, 128), (1, 32, 32, 160), (6, 0, 16, 192), (7, 0, 16, 208), (4, 32, 32, 224),
)


def layer(layout, blocks, wq, wkv, wo, cos, sin, allow):
    hbm = pl.BlockSpec(memory_space=pl.ANY)
    vmem = pl.BlockSpec(memory_space=pltpu.VMEM)
    return pl.pallas_call(
        functools.partial(layer_kernel, layout),
        out_shape=[jax.ShapeDtypeStruct((ROWS, WIDTH), BF16)] * 8,
        in_specs=[hbm] * (len(blocks) + 3) + [vmem] * 3,
        out_specs=[vmem] * 8,
        scratch_shapes=[
            pltpu.VMEM((2 * MB, WIDTH), BF16),
            pltpu.VMEM((WIDTH, QKV), BF16),
            pltpu.VMEM((HEADS * HEAD, WIDTH), BF16),
            pltpu.VMEM((2 * MB, QKV), F32),
            pltpu.VMEM((2 * MB, HEADS * HEAD), BF16),
            pltpu.SemaphoreType.DMA,
            pltpu.SemaphoreType.DMA((WIDTH // KC,)),
            pltpu.SemaphoreType.DMA((WIDTH // NC,)),
        ],
        compiler_params=pltpu.CompilerParams(vmem_limit_bytes=48 * 1024 * 1024),
        cost_estimate=pl.CostEstimate(flops=6 * 10**9, bytes_accessed=28 * 2**20, transcendentals=0),
        name="layer",
    )(*blocks, wq, wkv, wo, cos, sin, allow)


VC = 2048


def vocab_kernel(ids, order_ref, *refs):
    n = len(ids)
    blocks = refs[:n]
    w0_ref, w1_ref, want_ref = refs[n : n + 3]
    last = len(refs) > n + 9
    out_ref, rows, w, acc, row_sem, w_sem = refs[-6:]
    for i, b in enumerate(blocks):
        pltpu.make_async_copy(b, rows.at[pl.ds(i * ROWS, ROWS)], row_sem).start()

    @pl.loop(0, WIDTH // VC)
    def _(k):
        cols = at(k, VC)
        for i, r in enumerate((w0_ref, w1_ref)):
            pltpu.make_async_copy(r.at[cols], w.at[cols, pl.ds(i * VL, VL)], w_sem.at[k]).start()

    acc[...] = jnp.zeros_like(acc)
    pltpu.make_async_copy(rows, rows, row_sem).wait()

    @pl.loop(0, WIDTH // VC, unroll=True)
    def _(k):
        cols = at(k, VC)
        pltpu.make_async_copy(w.at[cols], w.at[cols], w_sem.at[k]).wait()
        acc[...] += jnp.dot(rows[:, cols], w[cols, :], preferred_element_type=F32)

    logits = acc[...]
    top = jnp.max(logits, axis=1, keepdims=True)
    total = jnp.sum(jnp.exp(logits - top), axis=1, keepdims=True)
    column = lax.broadcasted_iota(jnp.int32, logits.shape, 1)
    want = jnp.concatenate([want_ref[i * ROWS : (i + 1) * ROWS, :1] for i in ids], axis=0)
    picked = jnp.sum(jnp.where(column == want, logits, 0.0), axis=1, keepdims=True)
    lane = lax.broadcasted_iota(jnp.int32, (n * ROWS, 128), 1)
    stats = jnp.where(lane == 0, top, jnp.where(lane == 1, total, picked))
    if n < NZ:
        stats = jnp.concatenate([stats, jnp.zeros((MB - n * ROWS, 128), F32)], axis=0)
    if n * ROWS % MB and n > NZ:
        stats = jnp.concatenate([stats, jnp.zeros((2 * MB - n * ROWS, 128), F32)], axis=0)
    stats = stats.T
    if last:
        out_ref[:8, :] = refs[n + 3][...]
    for i, block in enumerate(ids):
        mine = slice(i * ROWS, (i + 1) * ROWS)
        line = jnp.concatenate([stats[k : k + 1, mine] for k in (0, 1, 2, 2)], axis=1)
        out_ref[pl.ds(order_ref[block], 1), :] = line
    if last:
        lines = out_ref[:8, :]
        for s in range(1, 16):
            out_ref[s * 8 : (s + 1) * 8, :] = lines


def vocab_part(ids, order, blocks, w0, w1, want, lines=None):
    hbm = pl.BlockSpec(memory_space=pl.ANY)
    vmem = pl.BlockSpec(memory_space=pltpu.VMEM)
    given = [] if lines is None else [lines]
    return pl.pallas_call(
        functools.partial(vocab_kernel, ids),
        out_shape=jax.ShapeDtypeStruct((128 if given else 8, 128), F32),
        in_specs=[pl.BlockSpec(memory_space=pltpu.SMEM)] + [hbm] * (len(ids) + 2) + [vmem] * (1 + len(given)),
        out_specs=vmem,
        scratch_shapes=[
            pltpu.VMEM((len(ids) * ROWS, WIDTH), BF16),
            pltpu.VMEM((WIDTH, 2 * VL), BF16),
            pltpu.VMEM((len(ids) * ROWS, 2 * VL), F32),
            pltpu.SemaphoreType.DMA,
            pltpu.SemaphoreType.DMA((WIDTH // VC,)),
        ],
        compiler_params=pltpu.CompilerParams(vmem_limit_bytes=32 * 1024 * 1024),
        cost_estimate=pl.CostEstimate(flops=10**9, bytes_accessed=10 * 2**20, transcendentals=0),
        name="vocab",
    )(order, *[blocks[i] for i in ids], w0, w1, want, *given)


def vocab(order, blocks, w0, w1, want):
    lines = vocab_part((0, 1, 2, 3, 4), order, blocks, w0, w1, want)
    return vocab_part((5, 6, 7), order, blocks, w0, w1, want, lines)


def add(*terms):
    return sum(t.astype(F32) for t in terms)


BESIDE = [(r, r ^ (2 * 8) ^ NZ) for r in range(128)]


def spread_from_last(final_rows, section):
    y, h = section // 4, section // 2 % 2

    def hop(to):
        return over_section(final_rows, [(15, sec(to, 1, 1))])

    up, down, across = hop(0), hop(2), hop(1)
    rows = jnp.where(y == 3, final_rows, jnp.where(y == 0, up, jnp.where(y == 2, down, across)))
    here = [(r, to) for r, to in BESIDE if r // 8 % 4 == 3]
    return jnp.where(h == 1, rows, lax.ppermute(rows, ("section", "tensor"), here))


def body(
    section_input, positions, attn_gain, w_query, w_keyval, w_out_proj, final_gain, w_vocab, targets
):
    section, rank = lax.axis_index("section"), lax.axis_index("tensor")
    core, x, z = section % 2, rank // NZ, rank % NZ
    my_rows = section_input[0]
    normed = rms_norm(my_rows, attn_gain[0])
    other_vocab = over_section(w_vocab, [(s, s ^ 1) for s in range(16)])

    zs = (z + jnp.arange(NZ)) % NZ

    def order_from(first_x):
        return (jnp.stack([first_x, 1 - first_x])[:, None] * NZ + zs[None, :]).reshape(-1)

    def tables():
        place = ((zs * ROWS)[:, None] + jnp.arange(ROWS)[None, :]).reshape(-1)
        pos = jnp.take(positions[0].reshape(8, ROWS), order_from(x), axis=0).reshape(-1)
        place2 = jnp.concatenate([place, place])
        frequency = ROPE_THETA ** (-jnp.arange(HEAD // 2, dtype=F32) * 2.0 / HEAD)
        angles = pos.astype(F32)[:, None] * frequency[None, :]
        cos, sin = jnp.cos(angles), jnp.sin(angles)
        cos = jnp.concatenate([cos, cos], axis=1)
        sin = jnp.concatenate([-sin, sin], axis=1)
        keys_at = place[None, :]
        allow = ((keys_at <= place2[:, None]) & (keys_at >= (place2 - pos)[:, None])).astype(F32)
        return cos, sin, allow

    odd = core == 1
    blank = jnp.zeros((ROWS, WIDTH), BF16)
    weights = (w_query[0], w_keyval[0].reshape(WIDTH, -1), w_out_proj[0])
    blocks, angles = lax.cond(
        odd, lambda: (gather_rows(normed)[1:], tables()), lambda: ((blank,) * 7, tables())
    )
    blocks = (normed, *blocks)

    def layer_rows(layout, blocks):
        terms = scatter_sum(layer(layout, blocks, *weights, *angles))
        return finish(my_rows, terms, final_gain)

    def odd_path():
        layer_out, final_rows = layer_rows(EACH, blocks)
        order = order_from(jnp.where(section // 2 % 2 == 1, x, 1 - x))
        starts = jnp.stack([section, section ^ 1]) * 8 * VL + rank * VL
        want = jnp.take(targets.reshape(8, ROWS), order, axis=0).reshape(-1)
        local = want[:, None] - starts[None, :]
        inside = (local >= 0) & (local < VL)
        want = jnp.max(jnp.where(inside, local + jnp.arange(2)[None, :] * VL, -1), axis=1)
        want = jnp.broadcast_to(want[:, None], (2 * MB, 128))
        all_rows = gather_rows(spread_from_last(final_rows, section))
        return layer_out, vocab(order, all_rows, w_vocab, other_vocab, want)

    def even_path():
        return layer_rows(PAIRED, gather_pairs(normed))[0], jnp.zeros((128, 128), F32)

    layer_out, stats = lax.cond(odd, odd_path, even_path)
    handed = over_section(layer_out[None], [(s, s + 1) for s in range(15)])
    got = lax.all_to_all(stats, ("section", "tensor"), 0, 0, tiled=True)
    return handed, merge(got)


def solution(mesh):
    placed = (
        P("section", "tensor", None),
        P("section", None),
        P("section", None),
        P("section", None, "tensor"),
        P("section", None, "tensor", None),
        P("section", "tensor", None),
        P(),
        P(None, ("section", "tensor")),
        P(),
    )
    return jax.shard_map(
        body,
        mesh=mesh,
        in_specs=placed,
        out_specs=(P("section", "tensor", None), P("tensor")),
        check_vma=False,
    )
```
